32 devices in a mesh: row: 8 (over y, x, core), team: 4 (over z).
Axes of the slice: x: 2, y: 2, z: 4, core: 2. Of those that a mesh axis runs over, the one named last changes fastest.
Arguments:
- features: bfloat16 [16384, 512], P('row'), may hold values from -6 to 6
- weight: bfloat16 [512, 512], replicated, may hold values from -0.25 to 0.25
- table: bfloat16 [8, 512], replicated, may hold values from -5 to 5
- labels: int32 [16384], P('row'), may hold values from 0 to 7
- label_mask: int32 [16384], P('row'), may hold values 0 or 1
- block_vals: bfloat16 [8, 4, 16, 128, 128], P('row', 'team'), may hold values from -0.25 to 0.25
- block_row: int32 [8, 4, 16], P('row', 'team'), may hold values from 0 to 15, as said below
- block_col: int32 [8, 4, 16], P('row', 'team'), may hold values from 0 to 31
- block_count: int32 [8, 4], P('row', 'team'), may hold values from 1 to 16, as said below
Outputs:
- output: bfloat16 [16384, 512], P(('row', 'team'))
- grad_weight: float32 [512, 512], replicated
- grad_features: bfloat16 [4, 4096, 512], P('team', 'row')
The draws below stay inside these ranges and needn't reach their ends.
Inputs may be any that keep to these rules, and one draw needn't show every extreme that they name: Within one [r, t] list the pairs (block_row, block_col) of all 16 slots are distinct. Only the first block_count[r, t] slots of a list are live; some [r, t] has exactly 16 live slots in every draw.
All inputs are finite; a program needn't handle non-finite values. No bound on the sum of `label_mask` on one device may be relied on, other than what follows from the above.
Results may differ from the reference program's by a relative error of at most 0.0059.
Values may be sent and summed in bfloat16 or wider, within the bound.
No kernel may reach another device: no remote copies, remote signals or barrier semaphores. Data moves between devices by JAX's collectives and lax.ppermute only.
A program may use at most 64 MiB of HBM per device.

```python
import math
import jax
import jax.numpy as jnp
from jax import lax

F = 512
CL = 8
SB = 16
KMAX = 16
PANEL_SLABS = 2
SLAB = 2048
NODES = 16384
N_ROW = 8
N_TEAM = 4


def block_layout(key):
    device_keys = jax.random.split(key, N_ROW * N_TEAM)
    shuffled = jax.vmap(lambda one_key: jax.random.permutation(one_key, PANEL_SLABS * SB * SB))(device_keys)
    return shuffled[:, :KMAX].reshape(N_ROW, N_TEAM, KMAX).astype(jnp.int32)


def draw_block_row(key, part):
    layout = block_layout(jax.random.fold_in(key, 7))
    return (layout // (PANEL_SLABS * SB)).astype(jnp.int32)


def draw_block_col(key, part):
    layout = block_layout(jax.random.fold_in(key, 7))
    return (layout % (PANEL_SLABS * SB)).astype(jnp.int32)


def draw_block_count(key, part):
    first_key, second_key, third_key = jax.random.split(jax.random.fold_in(key, 11), 3)
    devices = N_ROW * N_TEAM
    counts = jax.random.randint(first_key, (devices,), max(1, KMAX // 8), KMAX // 2 + 1)
    first_full = jax.random.randint(second_key, (), 0, devices)
    second_full = jax.random.randint(third_key, (), 0, devices)
    places = jnp.arange(devices, dtype=jnp.int32)
    counts = jnp.where((places == first_full) | (places == second_full), KMAX, counts)
    return counts.reshape(N_ROW, N_TEAM).astype(jnp.int32)


def touch_ends(drawn, stream_key, smallest, top_value):
    longest = drawn.shape.index(max(drawn.shape))
    spots = []
    for shift in (0, 1):
        where = [jax.random.randint(jax.random.fold_in(stream_key, axis), (), 0, length) for axis, length in enumerate(drawn.shape)]
        where[longest] = (where[longest] + shift) % drawn.shape[longest]
        spots.append(tuple(where))
    return drawn.at[spots[0]].set(smallest).at[spots[1]].set(top_value)


def levels(stream_key, dims, cuts, low, high):
    loudness, own = 1.0, jax.random.fold_in(stream_key, 6)
    for dim, shards_of in cuts:
        heights = jnp.exp(jax.random.uniform(jax.random.fold_in(own, dim), (shards_of,), jnp.float32, low / len(cuts), high / len(cuts)))
        loudness = loudness * jnp.repeat(heights, dims[dim] // shards_of).reshape([-1 if axis == dim else 1 for axis in range(len(dims))])
    return loudness


def centred(key, shape, deviation, reach, shards=(), kind=jnp.bfloat16):
    entries = jax.random.normal(key, shape, jnp.float32) * deviation
    if len(shards) > 0:
        entries = levels(key, shape, shards, -0.22, 0.18) * entries
    return jnp.clip(entries, min=-reach, max=reach).astype(kind)


def setup_inputs(seed: int = 0) -> dict:
    key_of = jax.random.split(jax.random.key(seed), 10)
    features = centred(key_of[0], (NODES, F), 1.0, 6.0, ((0, 8),))
    weight = centred(key_of[1], (F, F), F ** -0.5, 0.25)
    table = centred(key_of[2], (CL, F), 1.0, 5.0)
    labels = touch_ends(jax.random.randint(key_of[3], (NODES,), 0, CL), jax.random.fold_in(key_of[3], 1), 0, CL - 1).astype(jnp.int32)
    label_mask = touch_ends((jax.random.randint(key_of[4], (NODES,), 0, 2) < 1).astype(jnp.int32), jax.random.fold_in(key_of[4], 1), 0, 1)
    block_vals = centred(key_of[5], (N_ROW, N_TEAM, KMAX, 128, 128), (32 * KMAX) ** -0.5, 0.25, ((0, 8), (1, 4)))
    block_row = draw_block_row(jax.random.fold_in(key_of[9], 71), 0)
    block_col = draw_block_col(jax.random.fold_in(key_of[9], 71), 0)
    block_count = draw_block_count(jax.random.fold_in(key_of[9], 71), 0)
    return dict(features=features, weight=weight, table=table, labels=labels, label_mask=label_mask, block_vals=block_vals, block_row=block_row, block_col=block_col, block_count=block_count)


def silu_slope(preact):
    sigma = jax.nn.sigmoid(preact)
    return sigma * (1.0 + preact * (1.0 - sigma))

def reference(features, weight, table, labels, label_mask, block_vals, block_row, block_col, block_count):
    feature_width = features.shape[1]
    panel_rows = PANEL_SLABS * SLAB

    def forward_slab(slab_index):

        def team_part(totals, team_index):
            feature_panel = lax.dynamic_slice_in_dim(features, (team_index * panel_rows).astype(jnp.int32), panel_rows, 0)

            def add_block(position, inner):
                col_start = (block_col[slab_index, team_index, position] * 128).astype(jnp.int32)
                row_start = (block_row[slab_index, team_index, position] * 128).astype(jnp.int32)
                source = lax.dynamic_slice_in_dim(feature_panel, col_start, 128, 0)
                product = jnp.dot(block_vals[slab_index, team_index, position], source, preferred_element_type=jnp.float32)
                current = lax.dynamic_slice_in_dim(inner, row_start, 128, 0)
                return lax.dynamic_update_slice_in_dim(inner, current + product, row_start, 0)
            totals = lax.fori_loop(jnp.int32(0), block_count[slab_index, team_index], add_block, totals)
            return (totals, None)
        totals, unused = lax.scan(team_part, jnp.zeros((SLAB, feature_width), jnp.float32), jnp.arange(N_TEAM, dtype=jnp.int32))
        return totals
    agg = lax.map(forward_slab, jnp.arange(N_ROW, dtype=jnp.int32)).reshape(NODES, feature_width).astype(jnp.bfloat16)
    preact = jnp.dot(agg, weight, preferred_element_type=jnp.float32)
    active = jax.nn.silu(preact)
    output = active.astype(jnp.bfloat16)
    target = table.astype(jnp.float32)[labels]
    residual = label_mask.astype(jnp.float32)[:, None] * (active - target)
    grad_pre = (residual * silu_slope(preact)).astype(jnp.bfloat16)
    grad_weight = jnp.dot(agg.T, grad_pre, preferred_element_type=jnp.float32) * (1.0 / math.sqrt(NODES))
    back_rows = jnp.dot(grad_pre, weight.T, preferred_element_type=jnp.float32).astype(jnp.bfloat16)

    def backward_panel(team_index):

        def row_part(totals, slab_index):
            back_slab = lax.dynamic_slice_in_dim(back_rows, (slab_index * SLAB).astype(jnp.int32), SLAB, 0)

            def add_block(position, inner):
                col_start = (block_col[slab_index, team_index, position] * 128).astype(jnp.int32)
                row_start = (block_row[slab_index, team_index, position] * 128).astype(jnp.int32)
                source = lax.dynamic_slice_in_dim(back_slab, row_start, 128, 0)
                product = jnp.dot(block_vals[slab_index, team_index, position].T, source, preferred_element_type=jnp.float32)
                current = lax.dynamic_slice_in_dim(inner, col_start, 128, 0)
                return lax.dynamic_update_slice_in_dim(inner, current + product, col_start, 0)
            totals = lax.fori_loop(jnp.int32(0), block_count[slab_index, team_index], add_block, totals)
            return (totals, None)
        totals, unused = lax.scan(row_part, jnp.zeros((panel_rows, feature_width), jnp.float32), jnp.arange(N_ROW, dtype=jnp.int32))
        return totals
    grad_features = lax.map(backward_panel, jnp.arange(N_TEAM, dtype=jnp.int32)).astype(jnp.bfloat16)
    return (output, grad_weight, grad_features)
```

```python
import functools
import math

import jax
import jax.numpy as jnp
from jax import lax
from jax.experimental import pallas as pl
from jax.experimental.pallas import tpu as pltpu
from jax.sharding import PartitionSpec as P

BLOCK = 128
GROUP = 4
ID_ROWS = 16
MIB = 1 << 20


def lanes(width):
    return -(-width // 128) * 128


def swap(value, axis, flip):
    size = lax.axis_size(axis)
    return lax.ppermute(value, axis, [(i, i ^ flip) for i in range(size)])


def load_ids(ids_vmem, ids_smem, lists, slots, sem):
    for d in range(lists.shape[0]):
        rows = lists[d, slots * BLOCK :, :].astype(jnp.float32)
        ids_vmem[d] = rows.astype(jnp.int32)[:8]
    copy = pltpu.make_async_copy(ids_vmem, ids_smem, sem)
    copy.start()
    copy.wait()


def each_group(ids, place, teams, visit):
    for d in range(teams):
        live = ids[d, 2, 0]

        def step(group, carry, d=d, live=live):
            visit(d, place[0] ^ d, group * GROUP, live)
            return carry

        lax.fori_loop(0, (live + GROUP - 1) // GROUP, step, 0)


def forward_kernel(chips, teams, slots, place, *refs):
    near = refs[:chips]
    far = refs[chips : 2 * chips]
    given = refs[2 * chips : 2 * chips + teams]
    outs = refs[2 * chips + teams : 2 * chips + 2 * teams]
    panels, lists, totals, ids_vmem, ids_smem, sems, id_sem = refs[2 * chips + 2 * teams :]
    slab = near[0].shape[0]
    panel_rows = panels.shape[0] // teams
    share = slab // teams
    team, chip, core = place[0], place[1], place[2]
    copies = []
    for d in range(teams):
        copies.append(pltpu.make_async_copy(given[d], lists.at[d], sems.at[d]))
    for d in range(chips):
        for side, source in ((core, near[d]), (1 - core, far[d])):
            start = pl.multiple_of((2 * (chip ^ d) + side) * slab, slab)
            target = panels.at[pl.ds(start, slab), :]
            copies.append(pltpu.make_async_copy(source, target, sems.at[len(copies)]))
    for copy in copies:
        copy.start()
    totals[...] = jnp.zeros_like(totals)
    for copy in copies[:teams]:
        copy.wait()
    load_ids(ids_vmem, ids_smem, lists, slots, id_sem)
    for copy in copies[teams:]:
        copy.wait()

    def visit(d, panel, first, live):
        products = []
        for u in range(GROUP):
            slot = first + u
            start = panel * panel_rows + ids_smem[d, 1, slot] * BLOCK
            source = panels[pl.ds(pl.multiple_of(start, BLOCK), BLOCK), :]
            block = lists[d, pl.ds(pl.multiple_of(slot * BLOCK, BLOCK), BLOCK), :]
            product = jnp.dot(block, source, preferred_element_type=jnp.float32)
            products.append(jnp.where(slot < live, product, 0.0))
        for u in range(GROUP):
            start = pl.multiple_of(ids_smem[d, 0, first + u] * BLOCK, BLOCK)
            totals[pl.ds(start, BLOCK), :] += products[u]

    each_group(ids_smem, place, teams, visit)
    for d in range(teams):
        start = pl.multiple_of((team ^ d) * share, share)
        outs[d][...] = totals[pl.ds(start, share), :].astype(jnp.bfloat16)


def layer_kernel(teams, place, *refs):
    parts = refs[:teams]
    weight, table, labels, mask = refs[teams : teams + 4]
    output, grad_pre = refs[teams + 4 : teams + 6]
    backs = refs[teams + 6 :]
    team = place[0]
    width = parts[0].shape[1]

    def weight_rows(d):
        return weight[pl.ds(pl.multiple_of((team ^ d) * width, width), width), :]

    preact = jnp.dot(parts[0][...], weight_rows(0), preferred_element_type=jnp.float32)
    for d in range(1, teams):
        preact += jnp.dot(parts[d][...], weight_rows(d), preferred_element_type=jnp.float32)
    sigma = 1.0 / (1.0 + jnp.exp(-preact))
    active = preact * sigma
    output[...] = active.astype(jnp.bfloat16)
    classes = table.shape[0]
    row_labels = labels[pl.ds(team, 1), :]
    row_mask = mask[pl.ds(team, 1), :].astype(jnp.float32)
    rows = row_labels.shape[1]
    index = lax.broadcasted_iota(jnp.int32, (classes, rows), 0)
    known = jnp.where(index == row_labels, row_mask, 0.0).astype(jnp.bfloat16)
    held = jnp.broadcast_to(row_mask * (1.0 / 8.0), (8, rows)).astype(jnp.bfloat16)
    across = (((0,), (0,)), ((), ()))
    target = lax.dot_general(known, table[...], across, preferred_element_type=jnp.float32)
    ones = jnp.ones((8, table.shape[1]), jnp.bfloat16)
    masked = lax.dot_general(held, ones, across, preferred_element_type=jnp.float32)
    slope = sigma * (1.0 + preact * (1.0 - sigma))
    grad = ((masked * active - target) * slope).astype(jnp.bfloat16)
    grad_pre[...] = grad
    for d in range(teams):
        backs[d][...] = lax.dot_general(
            grad, weight_rows(d), (((1,), (1,)), ((), ())), preferred_element_type=jnp.float32
        ).astype(jnp.bfloat16)


def weight_kernel(teams, place, *refs):
    parts = refs[:teams]
    grad_pre, keep, send, term = refs[teams:]
    width = parts[0].shape[1]
    half = keep.shape[0]
    for d in range(teams):
        start = pl.multiple_of((place[0] ^ d) * width, width)
        term[pl.ds(start, width), :] = lax.dot_general(
            parts[d][...], grad_pre[...], (((0,), (0,)), ((), ())), preferred_element_type=jnp.float32
        )
    core = place[2]
    keep[...] = term[pl.ds(pl.multiple_of(core * half, half), half), :]
    send[...] = term[pl.ds(pl.multiple_of((1 - core) * half, half), half), :].astype(jnp.bfloat16)


def backward_kernel(chips, teams, slots, piece, place, *refs):
    given = refs[:teams]
    backs = refs[teams : 2 * teams]
    keep, send, lists, rows, totals, ids_vmem, ids_smem, sems, id_sem = refs[2 * teams :]
    team, core = place[0], place[2]
    share = backs[0].shape[0]
    per_piece = piece // BLOCK
    copies = []
    for d in range(teams):
        copies.append(pltpu.make_async_copy(given[d], lists.at[d], sems.at[d]))
    for d in range(teams):
        start = pl.multiple_of((team ^ d) * share, share)
        target = rows.at[pl.ds(start, share), :]
        copies.append(pltpu.make_async_copy(backs[d], target, sems.at[teams + d]))
    for copy in copies:
        copy.start()
    totals[...] = jnp.zeros_like(totals)
    for copy in copies[:teams]:
        copy.wait()
    load_ids(ids_vmem, ids_smem, lists, slots, id_sem)
    for copy in copies[teams:]:
        copy.wait()

    def visit(d, panel, first, live):
        products = []
        for u in range(GROUP):
            slot = first + u
            start = pl.multiple_of(ids_smem[d, 0, slot] * BLOCK, BLOCK)
            source = rows[pl.ds(start, BLOCK), :]
            block = lists[d, pl.ds(pl.multiple_of(slot * BLOCK, BLOCK), BLOCK), :]
            product = lax.dot_general(
                block, source, (((0,), (0,)), ((), ())), preferred_element_type=jnp.float32
            )
            products.append(jnp.where(slot < live, product, 0.0))
        for u in range(GROUP):
            col = ids_smem[d, 1, first + u]
            owner = col // per_piece
            slot_half = (owner % 2) ^ core
            slot_chip = owner // 2
            start = ((slot_half * chips + slot_chip) * teams + panel) * piece
            start = pl.multiple_of(start + (col % per_piece) * BLOCK, BLOCK)
            totals[pl.ds(start, BLOCK), :] += products[u]

    each_group(ids_smem, place, teams, visit)
    half = totals.shape[0] // 2
    keep[...] = totals[:half, :].astype(jnp.bfloat16)
    send[...] = totals[half:, :].astype(jnp.bfloat16)


def pair_kernel(chips, place, keep, taken, *outs):
    rows = outs[0].shape[0]
    for d in range(chips):
        here = pl.ds(pl.multiple_of((place[1] ^ d) * rows, rows), rows)
        total = keep[here, :].astype(jnp.float32) + taken[here, :].astype(jnp.float32)
        outs[d][...] = total.astype(jnp.bfloat16)


def plane_kernel(chips, teams, place, *refs):
    parts = refs[:chips]
    outs = refs[chips:]
    rows = outs[0].shape[0]
    for d in range(teams):
        here = pl.ds(pl.multiple_of((place[0] ^ d) * rows, rows), rows)
        total = parts[0][here, :].astype(jnp.float32)
        for part in parts[1:]:
            total += part[here, :].astype(jnp.float32)
        outs[d][...] = total.astype(jnp.bfloat16)


def join_kernel(teams, place, *refs):
    parts = refs[:teams]
    out, held = refs[teams:]
    width = parts[0].shape[1]
    for d in range(teams):
        held[place[0] ^ d] = parts[d][...]
    for d in range(teams):
        out[:, d * width : (d + 1) * width] = held[d]


def call(kernel, name, place, operands, spaces, out_shapes, scratch, flops, limit):
    moved = sum(math.prod(x.shape) * x.dtype.itemsize for x in (*operands, *out_shapes))
    specs = [pl.BlockSpec(memory_space=pltpu.SMEM)]
    specs += [pl.BlockSpec(memory_space=space) for space in spaces]
    return pl.pallas_call(
        kernel,
        name=name,
        in_specs=specs,
        out_specs=[pl.BlockSpec(memory_space=pltpu.VMEM) for _ in out_shapes],
        out_shape=out_shapes,
        scratch_shapes=scratch,
        cost_estimate=pl.CostEstimate(flops=flops, bytes_accessed=moved, transcendentals=0),
        compiler_params=pltpu.CompilerParams(vmem_limit_bytes=limit),
    )(place, *operands)


def per_device(
    features, weight, table, labels, label_mask, block_vals, block_row, block_col, block_count
):
    slab, width = features.shape
    slots = block_vals.shape[2]
    rows_n = lax.axis_size("row")
    teams = lax.axis_size("team")
    chips = rows_n // 2
    nodes = slab * rows_n
    part = width // teams
    share = slab // teams
    piece = nodes // teams // rows_n
    team = lax.axis_index("team")
    row = lax.axis_index("row")
    place = jnp.stack([team, row // 2, row % 2]).astype(jnp.int32)
    bf16 = jnp.bfloat16

    def shaped(*dims, kind=bf16):
        return jax.ShapeDtypeStruct(dims, kind)

    ids = jnp.zeros((ID_ROWS, BLOCK), jnp.int32)
    ids = ids.at[0, :slots].set(block_row[0, 0]).at[1, :slots].set(block_col[0, 0])
    ids = ids.at[2, 0].set(block_count[0, 0]).astype(bf16)
    mine = jnp.concatenate([block_vals.reshape(slots * BLOCK, BLOCK), ids], axis=0)
    lists = [mine] + [None] * (teams - 1)
    for d in sorted(range(1, teams), key=lambda d: -d):
        lists[d] = swap(mine, "team", d)
    near = [lax.dynamic_slice_in_dim(features, team * part, part, 1)]
    near += [swap(near[0], "row", 2 * d) for d in range(1, chips)]
    far = [swap(value, "row", 1) for value in near]

    any_space, vmem = pl.ANY, pltpu.VMEM
    padded = lanes(part)
    list_scratch = pltpu.VMEM((teams, slots * BLOCK + ID_ROWS, BLOCK), bf16)
    id_scratch = [
        pltpu.VMEM((teams, 8, BLOCK), jnp.int32),
        pltpu.SMEM((teams, 8, BLOCK), jnp.int32),
    ]
    list_bytes = teams * (slots * BLOCK + ID_ROWS) * BLOCK * 2
    product_flops = 2 * teams * slots * BLOCK * BLOCK * part
    sent = call(
        functools.partial(forward_kernel, chips, teams, slots),
        "forward",
        place,
        [*near, *far, *lists],
        [any_space] * (2 * chips + teams),
        [shaped(share, part)] * teams,
        [
            pltpu.VMEM((nodes, part), bf16),
            list_scratch,
            pltpu.VMEM((slab, part), jnp.float32),
            *id_scratch,
            pltpu.SemaphoreType.DMA((2 * chips + teams,)),
            pltpu.SemaphoreType.DMA,
        ],
        product_flops,
        nodes * padded * 2 + list_bytes + slab * padded * 8 + 4 * MIB,
    )
    aggs = [sent[0]] + [swap(sent[d], "team", d) for d in range(1, teams)]

    output, grad_pre, *backs = call(
        functools.partial(layer_kernel, teams),
        "layer",
        place,
        [*aggs, weight, table, labels.reshape(teams, share), label_mask.reshape(teams, share)],
        [vmem] * (teams + 4),
        [shaped(share, width)] * 2 + [shaped(share, part)] * teams,
        [],
        4 * share * width * width,
        16 * MIB,
    )
    backs = [backs[0]] + [swap(backs[d], "team", d) for d in range(1, teams)]

    half = width // 2
    w_keep, w_send = call(
        functools.partial(weight_kernel, teams),
        "weight_term",
        place,
        [*aggs, grad_pre],
        [vmem] * (teams + 1),
        [shaped(half, width, kind=jnp.float32), shaped(half, width)],
        [pltpu.VMEM((width, width), jnp.float32)],
        2 * share * width * width,
        12 * MIB,
    )
    w_pair = (w_keep + swap(w_send, "row", 1).astype(jnp.float32)).astype(bf16)
    w_rows = half // chips
    w_pieces = [
        lax.dynamic_slice_in_dim(w_pair, ((row // 2) ^ d) * w_rows, w_rows, 0) for d in range(chips)
    ]
    w_plane = w_pieces[0].astype(jnp.float32)
    for d in range(1, chips):
        w_plane = w_plane + swap(w_pieces[d], "row", 2 * d).astype(jnp.float32)
    w_plane = w_plane.astype(bf16)
    w_total = w_plane.astype(jnp.float32)
    for d in range(1, teams):
        w_total = w_total + swap(w_plane, "team", d).astype(jnp.float32)
    w_total = w_total * (1.0 / math.sqrt(nodes))
    w_half = jnp.zeros((half, width), jnp.float32)
    for d in range(chips):
        taken = swap(w_total, "row", 2 * d) if d else w_total
        w_half = lax.dynamic_update_slice_in_dim(w_half, taken, ((row // 2) ^ d) * w_rows, 0)
    w_other = swap(w_half, "row", 1)
    first = row % 2 == 0
    grad_weight = jnp.concatenate(
        [jnp.where(first, w_half, w_other), jnp.where(first, w_other, w_half)], axis=0
    )

    half_rows = nodes // 2
    keep, send = call(
        functools.partial(backward_kernel, chips, teams, slots, piece),
        "backward",
        place,
        [*lists, *backs],
        [any_space] * (2 * teams),
        [shaped(half_rows, part)] * 2,
        [
            list_scratch,
            pltpu.VMEM((slab, part), bf16),
            pltpu.VMEM((nodes, part), jnp.float32),
            *id_scratch,
            pltpu.SemaphoreType.DMA((2 * teams,)),
            pltpu.SemaphoreType.DMA,
        ],
        product_flops,
        nodes * padded * 6 + list_bytes + slab * padded * 2 + 4 * MIB,
    )
    pieces = call(
        functools.partial(pair_kernel, chips),
        "pair_sum",
        place,
        [keep, swap(send, "row", 1)],
        [vmem] * 2,
        [shaped(teams * piece, part)] * chips,
        [],
        half_rows * part,
        half_rows * padded * 6 + 4 * MIB,
    )
    parts = [pieces[0]] + [swap(pieces[d], "row", 2 * d) for d in range(1, chips)]
    slices = call(
        functools.partial(plane_kernel, chips, teams),
        "plane_sum",
        place,
        parts,
        [vmem] * chips,
        [shaped(piece, part)] * teams,
        [],
        half_rows * part,
        half_rows * padded * 4 + 4 * MIB,
    )
    taken = [slices[0]] + [swap(slices[d], "team", d) for d in range(1, teams)]
    (grad_features,) = call(
        functools.partial(join_kernel, teams),
        "join",
        place,
        taken,
        [vmem] * teams,
        [shaped(piece, width)],
        [pltpu.VMEM((teams, piece, part), bf16)],
        piece * width,
        teams * piece * padded * 8 + 4 * MIB,
    )
    return (output, grad_weight, grad_features[None])


def solution(mesh):
    placed = (
        P("row", None),
        P(),
        P(),
        P("row"),
        P("row"),
        P("row", "team", None, None, None),
        P("row", "team", None),
        P("row", "team", None),
        P("row", "team"),
    )
    return jax.shard_map(
        per_device,
        mesh=mesh,
        in_specs=placed,
        out_specs=(P(("row", "team"), None), P(), P("team", "row", None)),
        check_vma=False,
    )
```

```python
import functools
import math

import jax
import jax.numpy as jnp
from jax import lax
from jax.experimental import pallas as pl
from jax.experimental.pallas import tpu as pltpu
from jax.sharding import PartitionSpec as P

BLOCK = 128
GROUP = 4
ID_ROWS = 16
MIB = 1 << 20


def lanes(width):
    return -(-width // 128) * 128


def swap(value, axis, flip):
    size = lax.axis_size(axis)
    return lax.ppermute(value, axis, [(i, i ^ flip) for i in range(size)])


def load_ids(ids_vmem, ids_smem, lists, slots, sem):
    for d in range(lists.shape[0]):
        rows = lists[d, slots * BLOCK :, :].astype(jnp.float32)
        ids_vmem[d] = rows.astype(jnp.int32)[:8]
    copy = pltpu.make_async_copy(ids_vmem, ids_smem, sem)
    copy.start()
    copy.wait()


def each_group(ids, place, given, visit):
    for i, d in enumerate(given):
        live = ids[i, 2, 0]

        def step(group, carry, i=i, d=d, live=live):
            visit(i, place[0] ^ d, group * GROUP, live)
            return carry

        lax.fori_loop(0, (live + GROUP - 1) // GROUP, step, 0)


def fetch_late(place, teams, middle, relayed, target, sem):
    at_end = (place[0] == 0) | (place[0] == teams - 1)

    @pl.when(at_end)
    def _():
        pltpu.make_async_copy(relayed, target, sem).start()

    @pl.when(jnp.logical_not(at_end))
    def _():
        pltpu.make_async_copy(middle, target, sem).start()

    return pltpu.make_async_copy(middle, target, sem)


def forward_visit(panels, panel_rows, lists, ids, totals):
    def visit(i, panel, first, live):
        products = []
        for u in range(GROUP):
            slot = first + u
            start = panel * panel_rows + ids[i, 1, slot] * BLOCK
            source = panels[pl.ds(pl.multiple_of(start, BLOCK), BLOCK), :]
            block = lists[i, pl.ds(pl.multiple_of(slot * BLOCK, BLOCK), BLOCK), :]
            product = jnp.dot(block, source, preferred_element_type=jnp.float32)
            products.append(jnp.where(slot < live, product, 0.0))
        for u in range(GROUP):
            start = pl.multiple_of(ids[i, 0, first + u] * BLOCK, BLOCK)
            totals[pl.ds(start, BLOCK), :] += products[u]

    return visit


def prepare_kernel(slots, place, *refs):
    vals, row_ids, col_ids, count = refs[:4]
    rows, cols, lives, tail, sems = refs[-5:]
    mine = refs[4] if len(refs) == 10 else refs[5]
    blocks = slots * BLOCK
    moves = [(row_ids, rows), (col_ids, cols), (count, lives), (vals, mine.at[pl.ds(0, blocks), :])]
    if len(refs) > 10:
        features, near = refs[4], refs[6]
        width = near.shape[1]
        start = pl.multiple_of(place[0] * width, width)
        moves.append((features.at[:, pl.ds(start, width)], near))
    copies = [
        pltpu.make_async_copy(source, target, sems.at[i])
        for i, (source, target) in enumerate(moves)
    ]
    for copy in copies:
        copy.start()
    tail[...] = jnp.zeros_like(tail)
    for copy in copies[:3]:
        copy.wait()
    tail[0:1, 0:slots] = rows[...].astype(jnp.float32)
    tail[1:2, 0:slots] = cols[...].astype(jnp.float32)
    tail[2:3, 0:1] = lives[...].astype(jnp.float32)
    mine[pl.ds(blocks, ID_ROWS), :] = tail[...].astype(jnp.bfloat16)
    for copy in copies[3:]:
        copy.wait()


def early_kernel(chips, teams, slots, place, *refs):
    near = refs[:chips]
    far = refs[chips : 2 * chips]
    early = teams - 1
    given = refs[2 * chips : 2 * chips + early]
    weight, table = refs[2 * chips + early : 2 * chips + early + 2]
    totals, late_panel, *kept = refs[2 * chips + early + 2 : 2 * chips + early + 6]
    panels, lists, ids_vmem, ids_smem, sems, id_sem = refs[2 * chips + early + 6 :]
    slab = near[0].shape[0]
    panel_rows = panels.shape[0] // teams
    team, chip, core = place[0], place[1], place[2]
    copies = []
    for d in range(early):
        copies.append(pltpu.make_async_copy(given[d], lists.at[d], sems.at[d]))
    for d in range(chips):
        for side, source in ((core, near[d]), (1 - core, far[d])):
            start = pl.multiple_of((2 * (chip ^ d) + side) * slab, slab)
            target = panels.at[pl.ds(start, slab), :]
            copies.append(pltpu.make_async_copy(source, target, sems.at[len(copies)]))
    for source, target in zip((weight, table), kept):
        copies.append(pltpu.make_async_copy(source, target, sems.at[len(copies)]))
    for copy in copies:
        copy.start()
    totals[...] = jnp.zeros_like(totals)
    for copy in copies[:early]:
        copy.wait()
    load_ids(ids_vmem, ids_smem, lists, slots, id_sem)
    for copy in copies[early:]:
        copy.wait()
    visit = forward_visit(panels, panel_rows, lists, ids_smem, totals)
    each_group(ids_smem, place, range(early), visit)
    start = pl.multiple_of((team ^ early) * panel_rows, panel_rows)
    late_panel[...] = panels[pl.ds(start, panel_rows), :]


def late_kernel(teams, slots, place, *refs):
    middle, relayed, begun, panel = refs[:4]
    outs = refs[4 : 4 + teams]
    totals, lists, ids_vmem, ids_smem, sem, id_sem = refs[4 + teams :]
    fetch = fetch_late(place, teams, middle, relayed, lists.at[0], sem)
    totals[...] = begun[...]
    fetch.wait()
    load_ids(ids_vmem, ids_smem, lists, slots, id_sem)
    visit = forward_visit(panel, 0, lists, ids_smem, totals)
    each_group(ids_smem, place, [teams - 1], visit)
    share = outs[0].shape[0]
    for d in range(teams):
        start = pl.multiple_of((place[0] ^ d) * share, share)
        outs[d][...] = totals[pl.ds(start, share), :].astype(jnp.bfloat16)


def layer_kernel(teams, place, *refs):
    parts = refs[:teams]
    weight, table, *fixed = refs[teams : teams + 4]
    output, grad_pre = refs[teams + 4 : teams + 6]
    backs = refs[teams + 6 : 2 * teams + 6]
    labels, mask, sems = refs[2 * teams + 6 :]
    team = place[0]
    width = parts[0].shape[1]
    copies = [
        pltpu.make_async_copy(source, target, sems.at[i])
        for i, (source, target) in enumerate(zip(fixed, (labels, mask)))
    ]
    for copy in copies:
        copy.start()

    def weight_rows(d):
        return weight[pl.ds(pl.multiple_of((team ^ d) * width, width), width), :]

    preact = jnp.dot(parts[0][...], weight_rows(0), preferred_element_type=jnp.float32)
    for d in range(1, teams):
        preact += jnp.dot(parts[d][...], weight_rows(d), preferred_element_type=jnp.float32)
    sigma = 1.0 / (1.0 + jnp.exp(-preact))
    active = preact * sigma
    output[...] = active.astype(jnp.bfloat16)
    classes = table.shape[0]
    for copy in copies:
        copy.wait()
    row_labels = labels[pl.ds(team, 1), :]
    row_mask = mask[pl.ds(team, 1), :].astype(jnp.float32)
    rows = row_labels.shape[1]
    index = lax.broadcasted_iota(jnp.int32, (classes, rows), 0)
    known = jnp.where(index == row_labels, row_mask, 0.0).astype(jnp.bfloat16)
    held = jnp.broadcast_to(row_mask * (1.0 / 8.0), (8, rows)).astype(jnp.bfloat16)
    across = (((0,), (0,)), ((), ()))
    target = lax.dot_general(known, table[...], across, preferred_element_type=jnp.float32)
    ones = jnp.ones((8, table.shape[1]), jnp.bfloat16)
    masked = lax.dot_general(held, ones, across, preferred_element_type=jnp.float32)
    slope = sigma * (1.0 + preact * (1.0 - sigma))
    grad = ((masked * active - target) * slope).astype(jnp.bfloat16)
    grad_pre[...] = grad
    for d in range(teams):
        backs[d][...] = lax.dot_general(
            grad, weight_rows(d), (((1,), (1,)), ((), ())), preferred_element_type=jnp.float32
        ).astype(jnp.bfloat16)


def weight_kernel(teams, chips, place, *refs):
    parts = refs[:teams]
    grad_pre, keep, send, term = refs[teams:]
    width = parts[0].shape[1]
    for d in range(teams):
        start = pl.multiple_of((place[0] ^ d) * width, width)
        term[pl.ds(start, width), :] = lax.dot_general(
            parts[d][...], grad_pre[...], (((0,), (0,)), ((), ())), preferred_element_type=jnp.float32
        ).astype(jnp.bfloat16)
    half = term.shape[0] // 2
    rows = half // chips
    for out, side in ((keep, place[2]), (send, 1 - place[2])):
        for q in range(chips):
            held = pl.ds(pl.multiple_of(side * half + q * rows, rows), rows)
            for t in range(teams):
                start = (q * teams + t) * rows
                out[start : start + rows, :] = term[held, t * width : (t + 1) * width]


def tree(values):
    while len(values) > 1:
        values = [values[i] + values[i + 1] for i in range(0, len(values), 2)]
    return values[0]


def weight_total_kernel(teams, place, *refs):
    out = refs[teams]
    rows = out.shape[0]
    values = [ref[ref.shape[0] - rows :, :].astype(jnp.float32) for ref in refs[:teams]]
    out[...] = tree(values).astype(out.dtype)


def weight_half_kernel(chips, teams, place, *refs):
    out = refs[chips]
    rows = refs[0].shape[0] // teams
    width = refs[0].shape[1]
    for d in range(chips):
        held = pl.ds(pl.multiple_of((place[1] ^ d) * rows, rows), rows)
        for t in range(teams):
            out[held, t * width : (t + 1) * width] = refs[d][t * rows : (t + 1) * rows, :]


def whole_kernel(scale, place, mine, taken, out):
    rows = mine.shape[0]
    for value, here in ((mine, place[2]), (taken, 1 - place[2])):
        held = pl.ds(pl.multiple_of(here * rows, rows), rows)
        out[held, :] = value[...].astype(jnp.float32) * scale


def backward_kernel(chips, teams, slots, piece, chunk, riders, place, *refs):
    count = len(chunk)
    last = teams - 1 in chunk
    given = refs[: count + last]
    backs = refs[count + last : count + last + teams]
    refs = refs[count + last + teams :]
    rider_refs, refs = refs[:riders], refs[riders:]
    keep, send, lists, rows, totals, ids_vmem, ids_smem, sems, id_sem = refs
    team, core = place[0], place[2]
    share = backs[0].shape[0]
    per_piece = piece // BLOCK
    plain = count - last
    copies = []
    for i in range(plain):
        copies.append(pltpu.make_async_copy(given[i], lists.at[i], sems.at[i]))
        copies[-1].start()
    if last:
        target = lists.at[plain]
        copies.append(fetch_late(place, teams, *given[plain:], target, sems.at[plain]))
    moves = []
    for d in range(teams):
        start = pl.multiple_of((team ^ d) * share, share)
        target = rows.at[pl.ds(start, share), :]
        moves.append(pltpu.make_async_copy(backs[d], target, sems.at[count + d]))
        moves[-1].start()
    totals[...] = jnp.zeros_like(totals)
    for copy in copies:
        copy.wait()
    load_ids(ids_vmem, ids_smem, lists, slots, id_sem)
    for copy in moves:
        copy.wait()

    def visit(i, panel, first, live):
        products = []
        for u in range(GROUP):
            slot = first + u
            start = pl.multiple_of(ids_smem[i, 0, slot] * BLOCK, BLOCK)
            source = rows[pl.ds(start, BLOCK), :]
            block = lists[i, pl.ds(pl.multiple_of(slot * BLOCK, BLOCK), BLOCK), :]
            product = lax.dot_general(
                block, source, (((0,), (0,)), ((), ())), preferred_element_type=jnp.float32
            )
            products.append(jnp.where(slot < live, product, 0.0))
        for u in range(GROUP):
            col = ids_smem[i, 1, first + u]
            owner = col // per_piece
            slot_half = (owner % 2) ^ core
            slot_chip = owner // 2
            start = ((slot_half * chips + slot_chip) * count + i) * piece
            start = pl.multiple_of(start + (col % per_piece) * BLOCK, BLOCK)
            totals[pl.ds(start, BLOCK), :] += products[u]

    each_group(ids_smem, place, chunk, visit)
    size = count * piece
    step = keep.shape[0] // chips
    for side, out in enumerate((keep, send)):
        for q in range(chips):
            here = (side * chips + q) * size
            out[q * step : q * step + size, :] = totals[here : here + size, :].astype(jnp.bfloat16)
            if riders:
                more = step - size
                rider = rider_refs[side][q * more : (q + 1) * more, :]
                out[q * step + size : (q + 1) * step, :] = rider


def pair_kernel(chips, place, keep, taken, *outs):
    rows = outs[0].shape[0]
    for d in range(chips):
        here = pl.ds(pl.multiple_of((place[1] ^ d) * rows, rows), rows)
        total = keep[here, :].astype(jnp.float32) + taken[here, :].astype(jnp.float32)
        outs[d][...] = total.astype(jnp.bfloat16)


def plane_kernel(chips, count, place, *refs):
    parts, outs = refs[:chips], refs[chips:]
    rider = outs[count] if len(outs) > count else None
    rows = outs[0].shape[0] - (rider.shape[0] if rider is not None else 0)

    def total(here):
        value = parts[0][here, :].astype(jnp.float32)
        for part in parts[1:]:
            value += part[here, :].astype(jnp.float32)
        return value.astype(jnp.bfloat16)

    for i in range(count):
        outs[i][:rows, :] = total(slice(i * rows, (i + 1) * rows))
    if rider is not None:
        value = total(slice(count * rows, None))
        rider[...] = value
        for i in range(count):
            outs[i][rows:, :] = value


def join_kernel(teams, place, *refs):
    parts = refs[:teams]
    out, held = refs[teams:]
    width = parts[0].shape[1]
    for d in range(teams):
        held[place[0] ^ d] = parts[d][: held.shape[1], :]
    for d in range(teams):
        out[:, d * width : (d + 1) * width] = held[d]


def call(kernel, name, operands, spaces, out_shapes, scratch, flops, limit, after=()):
    moved = sum(math.prod(x.shape) * x.dtype.itemsize for x in (*operands, *out_shapes))
    specs = [pl.BlockSpec(memory_space=space) for space in spaces]
    specs += [pl.BlockSpec(memory_space=pl.ANY) for _ in after]
    given = len(operands)

    def body(*refs):
        row = lax.axis_index("row")
        place = (lax.axis_index("team"), row // 2, row % 2)
        kernel(place, *refs[:given], *refs[given + len(after) :])

    return pl.pallas_call(
        body,
        name=name,
        in_specs=specs,
        out_specs=[pl.BlockSpec(memory_space=pltpu.VMEM) for _ in out_shapes],
        out_shape=out_shapes,
        scratch_shapes=scratch,
        cost_estimate=pl.CostEstimate(flops=flops, bytes_accessed=moved, transcendentals=0),
        compiler_params=pltpu.CompilerParams(vmem_limit_bytes=limit),
    )(*operands, *after)


def gather_lists(mine, teams):
    if teams == 4:
        two = swap(mine, "team", 2)
        one = swap(mine, "team", 1)
        held, two = lax.optimization_barrier((mine, two))
        relayed = lax.ppermute(two, "team", [(2, 3), (1, 0)])
        middle = lax.ppermute(held, "team", [(1, 2), (2, 1)])
        return [mine, one, two], [middle, relayed]
    early = [mine] + [swap(mine, "team", d) for d in range(1, teams - 1)]
    last = swap(mine, "team", teams - 1)
    return early, [last, last]


def per_device(
    features, weight, table, labels, label_mask, block_vals, block_row, block_col, block_count
):
    slab, width = features.shape
    slots = block_vals.shape[2]
    rows_n = lax.axis_size("row")
    teams = lax.axis_size("team")
    chips = rows_n // 2
    nodes = slab * rows_n
    panel_rows = nodes // teams
    part = width // teams
    share = slab // teams
    piece = panel_rows // rows_n
    team = lax.axis_index("team")
    bf16, f32 = jnp.bfloat16, jnp.float32
    any_space, vmem = pl.ANY, pltpu.VMEM
    padded = lanes(part)
    payload = slots * BLOCK + ID_ROWS

    def shaped(*dims, kind=bf16):
        return jax.ShapeDtypeStruct(dims, kind)

    def id_scratch(count):
        return [
            pltpu.VMEM((count, payload, BLOCK), bf16),
            pltpu.VMEM((count, 8, BLOCK), jnp.int32),
            pltpu.SMEM((count, 8, BLOCK), jnp.int32),
        ]

    list_bytes = payload * BLOCK * 2
    list_flops = 2 * slots * BLOCK * BLOCK * part

    aligned = part % 128 == 0
    prepared = call(
        functools.partial(prepare_kernel, slots),
        "prepare",
        [
            block_vals.reshape(slots * BLOCK, BLOCK),
            block_row.reshape(1, slots),
            block_col.reshape(1, slots),
            block_count,
            *([features] if aligned else []),
        ],
        [pltpu.HBM] * (4 + aligned),
        [shaped(payload, BLOCK)] + [shaped(slab, part)] * aligned,
        [
            pltpu.VMEM((1, slots), jnp.int32),
            pltpu.VMEM((1, slots), jnp.int32),
            pltpu.VMEM((1, 1), jnp.int32),
            pltpu.VMEM((ID_ROWS, BLOCK), f32),
            pltpu.SemaphoreType.DMA((5,)),
        ],
        0,
        60 * MIB,
    )
    mine = prepared[0]
    own = prepared[1] if aligned else lax.dynamic_slice_in_dim(features, team * part, part, 1)
    early, late = gather_lists(mine, teams)
    near = [own] + [swap(own, "row", 2 * d) for d in range(1, chips)]
    far = [swap(value, "row", 1) for value in near]

    ids = id_scratch(teams - 1)
    begun, late_panel, weight_here, table_here = call(
        functools.partial(early_kernel, chips, teams, slots),
        "early_products",
        [*near, *far, *early, weight, table],
        [any_space] * (2 * chips + teams + 1),
        [
            shaped(slab, part, kind=f32),
            shaped(panel_rows, part),
            shaped(*weight.shape),
            shaped(*table.shape),
        ],
        [
            pltpu.VMEM((nodes, part), bf16),
            *ids,
            pltpu.SemaphoreType.DMA((2 * chips + teams + 1,)),
            pltpu.SemaphoreType.DMA,
        ],
        (teams - 1) * list_flops,
        (nodes + panel_rows) * padded * 2 + teams * list_bytes + slab * padded * 4 + 4 * MIB,
    )
    ids = id_scratch(1)
    sent = call(
        functools.partial(late_kernel, teams, slots),
        "late_products",
        [*late, begun, late_panel],
        [any_space, any_space, vmem, vmem],
        [shaped(share, part)] * teams,
        [
            pltpu.VMEM((slab, part), f32),
            *ids,
            pltpu.SemaphoreType.DMA,
            pltpu.SemaphoreType.DMA,
        ],
        list_flops,
        (panel_rows + 5 * slab) * padded * 2 + list_bytes + 3 * MIB,
    )
    aggs = [sent[0]] + [swap(sent[d], "team", d) for d in range(1, teams)]

    output, grad_pre, *backs = call(
        functools.partial(layer_kernel, teams),
        "layer",
        [
            *aggs,
            weight_here,
            table_here,
            labels.reshape(teams, share),
            label_mask.reshape(teams, share),
        ],
        [vmem] * (teams + 2) + [any_space] * 2,
        [shaped(share, width)] * 2 + [shaped(share, part)] * teams,
        [
            pltpu.VMEM((teams, share), jnp.int32),
            pltpu.VMEM((teams, share), jnp.int32),
            pltpu.SemaphoreType.DMA((2,)),
        ],
        4 * share * width * width,
        16 * MIB,
    )
    backs = [backs[0]] + [swap(backs[d], "team", d) for d in range(1, teams)]

    half = width // 2
    rider = half // chips * teams
    w_keep, w_send = call(
        functools.partial(weight_kernel, teams, chips),
        "weight_term",
        [*aggs, grad_pre],
        [vmem] * (teams + 1),
        [shaped(chips * rider, part)] * 2,
        [pltpu.VMEM((width, width), bf16)],
        2 * share * width * width,
        12 * MIB,
    )

    def plane_total(pieces):
        return [pieces[0]] + [swap(pieces[d], "row", 2 * d) for d in range(1, chips)]

    chunks = [list(range(teams // 2, teams)), list(range(teams // 2))]
    lists = early + late
    slices = [None] * teams
    held, paired = [], []
    for chunk in chunks:
        count = len(chunk)
        first = chunk is chunks[0]
        rows = chips * count * piece
        moved = rows + first * chips * rider
        given = [lists[d] for d in chunk] + (lists[-1:] if teams - 1 in chunk else [])
        riders = [w_keep, w_send] if first else []
        held.append(
            call(
                functools.partial(
                    backward_kernel, chips, teams, slots, piece, chunk, len(riders)
                ),
                "backward",
                [*given, *backs, *riders],
                [any_space] * (len(given) + teams) + [vmem] * len(riders),
                [shaped(moved, part)] * 2,
                [
                    id_scratch(count)[0],
                    pltpu.VMEM((slab, part), bf16),
                    pltpu.VMEM((2 * rows, part), f32),
                    *id_scratch(count)[1:],
                    pltpu.SemaphoreType.DMA((count + teams,)),
                    pltpu.SemaphoreType.DMA,
                ],
                count * list_flops,
                rows * padded * 14 + count * list_bytes + slab * padded * 2 + 4 * MIB,
                after=[value[0] for value in held],
            )
        )
    mark = [held[1][0]]
    for chunk, (keep, send) in zip(chunks, held):
        moved = keep.shape[0]
        paired.append(
            call(
                functools.partial(pair_kernel, chips),
                "pair_sum",
                [keep, swap(send, "row", 1)],
                [vmem] * 2,
                [shaped(moved // chips, part)] * chips,
                [],
                moved * part,
                moved * padded * 6 + 3 * MIB,
                after=mark,
            )
        )
        mark = paired[0][:1]
    mark = paired[1][:1]
    for chunk, pieces in zip(chunks, paired):
        count = len(chunk)
        first = chunk is chunks[0]
        outs = [shaped(piece + first * rider, part)] * count + [shaped(rider, part)] * first
        sums = call(
            functools.partial(plane_kernel, chips, count),
            "plane_sum",
            plane_total(pieces),
            [vmem] * chips,
            outs,
            [],
            chips * count * piece * part,
            chips * (count * piece + rider) * padded * 4 + 3 * MIB,
            after=mark,
        )
        for d, value in zip(chunk, sums):
            slices[d] = swap(value, "team", d) if d else value
        mark = []
        if first:
            w_plane = sums[count]
    w_parts = [w_plane] + [
        slices[d] if d in chunks[0] else swap(w_plane, "team", d) for d in range(1, teams)
    ]
    (w_total,) = call(
        functools.partial(weight_total_kernel, teams),
        "weight_total",
        w_parts,
        [vmem] * teams,
        [shaped(rider, part)],
        [],
        half * width,
        6 * MIB,
        after=sums[:1],
    )
    (w_half,) = call(
        functools.partial(weight_half_kernel, chips, teams),
        "weight_half",
        plane_total([w_total] * chips),
        [vmem] * chips,
        [shaped(half, width)],
        [],
        half * width,
        6 * MIB,
        after=[slices[d] for d in chunks[1][1:]],
    )
    (grad_weight,) = call(
        functools.partial(whole_kernel, 1.0 / math.sqrt(nodes)),
        "weight_whole",
        [w_half, swap(w_half, "row", 1)],
        [vmem] * 2,
        [shaped(width, width, kind=f32)],
        [],
        half * width,
        6 * MIB,
    )
    (grad_features,) = call(
        functools.partial(join_kernel, teams),
        "join",
        slices,
        [vmem] * teams,
        [shaped(piece, width)],
        [pltpu.VMEM((teams, piece, part), bf16)],
        piece * width,
        teams * piece * padded * 8 + 3 * MIB,
    )

    return (output, grad_weight, grad_features[None])


def solution(mesh):
    placed = (
        P("row", None),
        P(),
        P(),
        P("row"),
        P("row"),
        P("row", "team", None, None, None),
        P("row", "team", None),
        P("row", "team", None),
        P("row", "team"),
    )
    return jax.shard_map(
        per_device,
        mesh=mesh,
        in_specs=placed,
        out_specs=(P(("row", "team"), None), P(), P("team", "row", None)),
        check_vma=False,
    )
```

```python
import functools
import math

import jax
import jax.numpy as jnp
from jax import lax
from jax.experimental import pallas as pl
from jax.experimental.pallas import tpu as pltpu
from jax.sharding import PartitionSpec as P

BLOCK = 128
GROUP = 4
ID_ROWS = 16
MIB = 1 << 20


def lanes(width):
    return -(-width // 128) * 128


def swap(value, axis, flip):
    size = lax.axis_size(axis)
    return lax.ppermute(value, axis, [(i, i ^ flip) for i in range(size)])


def load_ids(ids_vmem, ids_smem, lists, slots, sem, meanwhile):
    for d in range(lists.shape[0]):
        rows = lists[d, slots * BLOCK :, :].astype(jnp.float32)
        ids_vmem[d] = rows.astype(jnp.int32)[:8]
    copy = pltpu.make_async_copy(ids_vmem, ids_smem, sem)
    copy.start()
    meanwhile()
    copy.wait()


def each_group(ids, place, given, visit):
    for i, d in enumerate(given):
        live = ids[i, 2, 0]

        def step(group, carry, i=i, d=d, live=live):
            visit(i, place[0] ^ d, group * GROUP, live)
            return carry

        lax.fori_loop(0, (live + GROUP - 1) // GROUP, step, 0)


def fetch_late(place, teams, middle, relayed, target, sem):
    at_end = (place[0] == 0) | (place[0] == teams - 1)

    @pl.when(at_end)
    def _():
        pltpu.make_async_copy(relayed, target, sem).start()

    @pl.when(jnp.logical_not(at_end))
    def _():
        pltpu.make_async_copy(middle, target, sem).start()

    return pltpu.make_async_copy(middle, target, sem)


def forward_visit(panels, panel_rows, lists, ids, totals):
    def visit(i, panel, first, live):
        products = []
        for u in range(GROUP):
            slot = first + u
            start = panel * panel_rows + ids[i, 1, slot] * BLOCK
            source = panels[pl.ds(pl.multiple_of(start, BLOCK), BLOCK), :]
            block = lists[i, pl.ds(pl.multiple_of(slot * BLOCK, BLOCK), BLOCK), :]
            product = jnp.dot(block, source, preferred_element_type=jnp.float32)
            products.append(jnp.where(slot < live, product, 0.0))
        for u in range(GROUP):
            start = pl.multiple_of(ids[i, 0, first + u] * BLOCK, BLOCK)
            totals[pl.ds(start, BLOCK), :] += products[u]

    return visit


def prepare_kernel(slots, place, *refs):
    vals, row_ids, col_ids, count = refs[:4]
    rows, cols, lives, tail, sems = refs[-5:]
    mine = refs[4] if len(refs) == 10 else refs[5]
    blocks = slots * BLOCK
    moves = [(row_ids, rows), (col_ids, cols), (count, lives), (vals, mine.at[pl.ds(0, blocks), :])]
    if len(refs) > 10:
        features, near = refs[4], refs[6]
        width = near.shape[1]
        start = pl.multiple_of(place[0] * width, width)
        moves.append((features.at[:, pl.ds(start, width)], near))
    copies = [
        pltpu.make_async_copy(source, target, sems.at[i])
        for i, (source, target) in enumerate(moves)
    ]
    for copy in copies:
        copy.start()
    tail[...] = jnp.zeros_like(tail)
    for copy in copies[:3]:
        copy.wait()
    tail[0:1, 0:slots] = rows[...].astype(jnp.float32)
    tail[1:2, 0:slots] = cols[...].astype(jnp.float32)
    tail[2:3, 0:1] = lives[...].astype(jnp.float32)
    mine[pl.ds(blocks, ID_ROWS), :] = tail[...].astype(jnp.bfloat16)
    for copy in copies[3:]:
        copy.wait()


def early_kernel(chips, teams, slots, place, *refs):
    near = refs[:chips]
    far = refs[chips : 2 * chips]
    early = teams - 1
    given = refs[2 * chips : 2 * chips + early]
    weight, table = refs[2 * chips + early : 2 * chips + early + 2]
    totals, late_panel, *kept = refs[2 * chips + early + 2 : 2 * chips + early + 6]
    panels, lists, ids_vmem, ids_smem, sems, id_sem = refs[2 * chips + early + 6 :]
    slab = near[0].shape[0]
    panel_rows = panels.shape[0] // teams
    team, chip, core = place[0], place[1], place[2]
    copies = []
    for d in range(early):
        copies.append(pltpu.make_async_copy(given[d], lists.at[d], sems.at[d]))
    for d in range(chips):
        for side, source in ((core, near[d]), (1 - core, far[d])):
            start = pl.multiple_of((2 * (chip ^ d) + side) * slab, slab)
            target = panels.at[pl.ds(start, slab), :]
            copies.append(pltpu.make_async_copy(source, target, sems.at[len(copies)]))
    for source, target in zip((weight, table), kept):
        copies.append(pltpu.make_async_copy(source, target, sems.at[len(copies)]))
    for copy in copies:
        copy.start()

    def clear():
        totals[...] = jnp.zeros_like(totals)

    for copy in copies[:early]:
        copy.wait()
    load_ids(ids_vmem, ids_smem, lists, slots, id_sem, clear)
    for copy in copies[early:]:
        copy.wait()
    visit = forward_visit(panels, panel_rows, lists, ids_smem, totals)
    each_group(ids_smem, place, range(early), visit)
    start = pl.multiple_of((team ^ early) * panel_rows, panel_rows)
    late_panel[...] = panels[pl.ds(start, panel_rows), :]


def late_kernel(teams, slots, place, *refs):
    middle, relayed, begun, panel = refs[:4]
    outs = refs[4 : 4 + teams]
    totals, lists, ids_vmem, ids_smem, sem, id_sem = refs[4 + teams :]
    fetch = fetch_late(place, teams, middle, relayed, lists.at[0], sem)

    def take():
        totals[...] = begun[...]

    fetch.wait()
    load_ids(ids_vmem, ids_smem, lists, slots, id_sem, take)
    visit = forward_visit(panel, 0, lists, ids_smem, totals)
    each_group(ids_smem, place, [teams - 1], visit)
    share = outs[0].shape[0]
    for d in range(teams):
        start = pl.multiple_of((place[0] ^ d) * share, share)
        outs[d][...] = totals[pl.ds(start, share), :].astype(jnp.bfloat16)


def layer_kernel(teams, place, *refs):
    parts = refs[:teams]
    weight, table, *fixed = refs[teams : teams + 4]
    output, grad_pre = refs[teams + 4 : teams + 6]
    backs = refs[teams + 6 : 2 * teams + 6]
    labels, mask, sems = refs[2 * teams + 6 :]
    team = place[0]
    width = parts[0].shape[1]
    copies = [
        pltpu.make_async_copy(source, target, sems.at[i])
        for i, (source, target) in enumerate(zip(fixed, (labels, mask)))
    ]
    for copy in copies:
        copy.start()

    def weight_rows(d):
        return weight[pl.ds(pl.multiple_of((team ^ d) * width, width), width), :]

    preact = jnp.dot(parts[0][...], weight_rows(0), preferred_element_type=jnp.float32)
    for d in range(1, teams):
        preact += jnp.dot(parts[d][...], weight_rows(d), preferred_element_type=jnp.float32)
    sigma = 1.0 / (1.0 + jnp.exp(-preact))
    active = preact * sigma
    output[...] = active.astype(jnp.bfloat16)
    classes = table.shape[0]
    for copy in copies:
        copy.wait()
    row_labels = labels[pl.ds(team, 1), :]
    row_mask = mask[pl.ds(team, 1), :].astype(jnp.float32)
    rows = row_labels.shape[1]
    index = lax.broadcasted_iota(jnp.int32, (classes, rows), 0)
    known = jnp.where(index == row_labels, row_mask, 0.0).astype(jnp.bfloat16)
    held = jnp.broadcast_to(row_mask * (1.0 / 8.0), (8, rows)).astype(jnp.bfloat16)
    across = (((0,), (0,)), ((), ()))
    target = lax.dot_general(known, table[...], across, preferred_element_type=jnp.float32)
    ones = jnp.ones((8, table.shape[1]), jnp.bfloat16)
    masked = lax.dot_general(held, ones, across, preferred_element_type=jnp.float32)
    slope = sigma * (1.0 + preact * (1.0 - sigma))
    grad = ((masked * active - target) * slope).astype(jnp.bfloat16)
    grad_pre[...] = grad
    for d in range(teams):
        backs[d][...] = lax.dot_general(
            grad, weight_rows(d), (((1,), (1,)), ((), ())), preferred_element_type=jnp.float32
        ).astype(jnp.bfloat16)


def weight_kernel(teams, chips, place, *refs):
    parts = refs[:teams]
    grad_pre, keep, send, term = refs[teams:]
    width = parts[0].shape[1]
    for d in range(teams):
        start = pl.multiple_of((place[0] ^ d) * width, width)
        term[pl.ds(start, width), :] = lax.dot_general(
            parts[d][...], grad_pre[...], (((0,), (0,)), ((), ())), preferred_element_type=jnp.float32
        ).astype(jnp.bfloat16)
    half = term.shape[0] // 2
    rows = half // chips
    for out, side in ((keep, place[2]), (send, 1 - place[2])):
        for q in range(chips):
            held = pl.ds(pl.multiple_of(side * half + q * rows, rows), rows)
            for t in range(teams):
                start = (q * teams + t) * rows
                out[start : start + rows, :] = term[held, t * width : (t + 1) * width]


def tree(values):
    while len(values) > 1:
        values = [values[i] + values[i + 1] for i in range(0, len(values), 2)]
    return values[0]


def weight_total_kernel(teams, place, *refs):
    out = refs[teams]
    rows = out.shape[0]
    values = [ref[ref.shape[0] - rows :, :].astype(jnp.float32) for ref in refs[:teams]]
    out[...] = tree(values).astype(out.dtype)


def weight_half_kernel(chips, teams, place, *refs):
    out = refs[chips]
    rows = refs[0].shape[0] // teams
    width = refs[0].shape[1]
    for d in range(chips):
        held = pl.ds(pl.multiple_of((place[1] ^ d) * rows, rows), rows)
        for t in range(teams):
            out[held, t * width : (t + 1) * width] = refs[d][t * rows : (t + 1) * rows, :]


def whole_kernel(scale, place, mine, taken, out):
    rows = mine.shape[0]
    for value, here in ((mine, place[2]), (taken, 1 - place[2])):
        held = pl.ds(pl.multiple_of(here * rows, rows), rows)
        out[held, :] = value[...].astype(jnp.float32) * scale


def backward_kernel(chips, teams, slots, piece, chunk, riders, place, *refs):
    count = len(chunk)
    last = teams - 1 in chunk
    given = refs[: count + last]
    backs = refs[count + last : count + last + teams]
    refs = refs[count + last + teams :]
    rider_refs, refs = refs[:riders], refs[riders:]
    keep, send, lists, rows, totals, ids_vmem, ids_smem, sems, id_sem = refs
    team, core = place[0], place[2]
    share = backs[0].shape[0]
    per_piece = piece // BLOCK
    plain = count - last
    copies = []
    for i in range(plain):
        copies.append(pltpu.make_async_copy(given[i], lists.at[i], sems.at[i]))
        copies[-1].start()
    if last:
        target = lists.at[plain]
        copies.append(fetch_late(place, teams, *given[plain:], target, sems.at[plain]))
    moves = []
    for d in range(teams):
        start = pl.multiple_of((team ^ d) * share, share)
        target = rows.at[pl.ds(start, share), :]
        moves.append(pltpu.make_async_copy(backs[d], target, sems.at[count + d]))
        moves[-1].start()

    def clear():
        totals[...] = jnp.zeros_like(totals)

    for copy in copies:
        copy.wait()
    load_ids(ids_vmem, ids_smem, lists, slots, id_sem, clear)
    for copy in moves:
        copy.wait()

    def visit(i, panel, first, live):
        products = []
        for u in range(GROUP):
            slot = first + u
            start = pl.multiple_of(ids_smem[i, 0, slot] * BLOCK, BLOCK)
            source = rows[pl.ds(start, BLOCK), :]
            block = lists[i, pl.ds(pl.multiple_of(slot * BLOCK, BLOCK), BLOCK), :]
            product = lax.dot_general(
                block, source, (((0,), (0,)), ((), ())), preferred_element_type=jnp.float32
            )
            products.append(jnp.where(slot < live, product, 0.0))
        for u in range(GROUP):
            col = ids_smem[i, 1, first + u]
            owner = col // per_piece
            slot_half = (owner % 2) ^ core
            slot_chip = owner // 2
            start = ((slot_half * chips + slot_chip) * count + i) * piece
            start = pl.multiple_of(start + (col % per_piece) * BLOCK, BLOCK)
            totals[pl.ds(start, BLOCK), :] += products[u]

    each_group(ids_smem, place, chunk, visit)
    size = count * piece
    step = keep.shape[0] // chips
    for side, out in enumerate((keep, send)):
        for q in range(chips):
            here = (side * chips + q) * size
            out[q * step : q * step + size, :] = totals[here : here + size, :].astype(jnp.bfloat16)
            if riders:
                more = step - size
                rider = rider_refs[side][q * more : (q + 1) * more, :]
                out[q * step + size : (q + 1) * step, :] = rider


def pair_kernel(chips, place, keep, taken, *outs):
    rows = outs[0].shape[0]
    for d in range(chips):
        here = pl.ds(pl.multiple_of((place[1] ^ d) * rows, rows), rows)
        total = keep[here, :].astype(jnp.float32) + taken[here, :].astype(jnp.float32)
        outs[d][...] = total.astype(jnp.bfloat16)


def plane_kernel(chips, count, place, *refs):
    parts, outs = refs[:chips], refs[chips:]
    rider = outs[count] if len(outs) > count else None
    rows = outs[0].shape[0] - (rider.shape[0] if rider is not None else 0)

    def total(here):
        value = parts[0][here, :].astype(jnp.float32)
        for part in parts[1:]:
            value += part[here, :].astype(jnp.float32)
        return value.astype(jnp.bfloat16)

    for i in range(count):
        outs[i][:rows, :] = total(slice(i * rows, (i + 1) * rows))
    if rider is not None:
        value = total(slice(count * rows, None))
        rider[...] = value
        for i in range(count):
            outs[i][rows:, :] = value


def join_kernel(teams, place, *refs):
    parts = refs[:teams]
    out, held = refs[teams:]
    width = parts[0].shape[1]
    for d in range(teams):
        held[place[0] ^ d] = parts[d][: held.shape[1], :]
    for d in range(teams):
        out[:, d * width : (d + 1) * width] = held[d]


def call(kernel, name, operands, spaces, out_shapes, scratch, flops, limit, after=()):
    moved = sum(math.prod(x.shape) * x.dtype.itemsize for x in (*operands, *out_shapes))
    specs = [pl.BlockSpec(memory_space=space) for space in spaces]
    specs += [pl.BlockSpec(memory_space=pl.ANY) for _ in after]
    given = len(operands)

    def body(*refs):
        row = lax.axis_index("row")
        place = (lax.axis_index("team"), row // 2, row % 2)
        kernel(place, *refs[:given], *refs[given + len(after) :])

    return pl.pallas_call(
        body,
        name=name,
        in_specs=specs,
        out_specs=[pl.BlockSpec(memory_space=pltpu.VMEM) for _ in out_shapes],
        out_shape=out_shapes,
        scratch_shapes=scratch,
        cost_estimate=pl.CostEstimate(
            flops=flops, bytes_accessed=moved if flops else 0, transcendentals=0
        ),
        compiler_params=pltpu.CompilerParams(vmem_limit_bytes=limit),
    )(*operands, *after)


def gather_lists(mine, teams, gate):
    if teams == 4:
        two = swap(mine, "team", 2)
        one = swap(mine, "team", 1)
        relayed = lax.ppermute(two, "team", [(2, 3), (1, 0)])
        held, _ = lax.optimization_barrier((mine, gate(two, one)))
        middle = lax.ppermute(held, "team", [(1, 2), (2, 1)])
        return [mine, one, two], [middle, relayed]
    early = [mine] + [swap(mine, "team", d) for d in range(1, teams - 1)]
    last = swap(mine, "team", teams - 1)
    return early, [last, last]


def per_device(
    features, weight, table, labels, label_mask, block_vals, block_row, block_col, block_count
):
    slab, width = features.shape
    slots = block_vals.shape[2]
    rows_n = lax.axis_size("row")
    teams = lax.axis_size("team")
    chips = rows_n // 2
    nodes = slab * rows_n
    panel_rows = nodes // teams
    part = width // teams
    share = slab // teams
    piece = panel_rows // rows_n
    team = lax.axis_index("team")
    bf16, f32 = jnp.bfloat16, jnp.float32
    any_space, vmem = pl.ANY, pltpu.VMEM
    padded = lanes(part)
    payload = slots * BLOCK + ID_ROWS

    def shaped(*dims, kind=bf16):
        return jax.ShapeDtypeStruct(dims, kind)

    def id_scratch(count):
        return [
            pltpu.VMEM((count, payload, BLOCK), bf16),
            pltpu.VMEM((count, 8, BLOCK), jnp.int32),
            pltpu.SMEM((count, 8, BLOCK), jnp.int32),
        ]

    list_bytes = payload * BLOCK * 2
    list_flops = 2 * slots * BLOCK * BLOCK * part

    aligned = part % 128 == 0
    prepared = call(
        functools.partial(prepare_kernel, slots),
        "prepare",
        [
            block_vals.reshape(slots * BLOCK, BLOCK),
            block_row.reshape(1, slots),
            block_col.reshape(1, slots),
            block_count,
            *([features] if aligned else []),
        ],
        [pltpu.HBM] * (4 + aligned),
        [shaped(payload, BLOCK)] + [shaped(slab, part)] * aligned,
        [
            pltpu.VMEM((1, slots), jnp.int32),
            pltpu.VMEM((1, slots), jnp.int32),
            pltpu.VMEM((1, 1), jnp.int32),
            pltpu.VMEM((ID_ROWS, BLOCK), f32),
            pltpu.SemaphoreType.DMA((5,)),
        ],
        0,
        60 * MIB,
    )
    mine = prepared[0]
    own = prepared[1] if aligned else lax.dynamic_slice_in_dim(features, team * part, part, 1)
    beside = swap(own, "row", 1)
    own, beside = lax.optimization_barrier((own, beside))
    near = [own] + [swap(own, "row", 2 * d) for d in range(1, chips)]
    early, late = gather_lists(mine, teams, lambda two, one: one)
    far = [beside] + [swap(value, "row", 1) for value in near[1:]]

    ids = id_scratch(teams - 1)
    begun, late_panel, weight_here, table_here = call(
        functools.partial(early_kernel, chips, teams, slots),
        "early_products",
        [*near, *far, *early, weight, table],
        [any_space] * (2 * chips + teams + 1),
        [
            shaped(slab, part, kind=f32),
            shaped(panel_rows, part),
            shaped(*weight.shape),
            shaped(*table.shape),
        ],
        [
            pltpu.VMEM((nodes, part), bf16),
            *ids,
            pltpu.SemaphoreType.DMA((2 * chips + teams + 1,)),
            pltpu.SemaphoreType.DMA,
        ],
        0,
        (nodes + panel_rows) * padded * 2 + teams * list_bytes + slab * padded * 4 + 4 * MIB,
    )
    ids = id_scratch(1)
    sent = call(
        functools.partial(late_kernel, teams, slots),
        "late_products",
        [*late, begun, late_panel],
        [any_space, any_space, vmem, vmem],
        [shaped(share, part)] * teams,
        [
            pltpu.VMEM((slab, part), f32),
            *ids,
            pltpu.SemaphoreType.DMA,
            pltpu.SemaphoreType.DMA,
        ],
        list_flops,
        (panel_rows + 5 * slab) * padded * 2 + list_bytes + 3 * MIB,
    )
    aggs = [sent[0]] + [swap(sent[d], "team", d) for d in range(1, teams)]

    output, grad_pre, *backs = call(
        functools.partial(layer_kernel, teams),
        "layer",
        [
            *aggs,
            weight_here,
            table_here,
            labels.reshape(teams, share),
            label_mask.reshape(teams, share),
        ],
        [vmem] * (teams + 2) + [any_space] * 2,
        [shaped(share, width)] * 2 + [shaped(share, part)] * teams,
        [
            pltpu.VMEM((teams, share), jnp.int32),
            pltpu.VMEM((teams, share), jnp.int32),
            pltpu.SemaphoreType.DMA((2,)),
        ],
        4 * share * width * width,
        16 * MIB,
    )
    backs = [backs[0]] + [swap(backs[d], "team", d) for d in range(1, teams)]

    half = width // 2
    rider = half // chips * teams
    w_keep, w_send = call(
        functools.partial(weight_kernel, teams, chips),
        "weight_term",
        [*aggs, grad_pre],
        [vmem] * (teams + 1),
        [shaped(chips * rider, part)] * 2,
        [pltpu.VMEM((width, width), bf16)],
        2 * share * width * width,
        12 * MIB,
    )

    def plane_total(pieces):
        return [pieces[0]] + [swap(pieces[d], "row", 2 * d) for d in range(1, chips)]

    chunks = [list(range(teams // 2, teams)), list(range(teams // 2))]
    lists = early + late
    slices = [None] * teams
    held, paired = [], []
    for chunk in chunks:
        count = len(chunk)
        first = chunk is chunks[0]
        rows = chips * count * piece
        moved = rows + first * chips * rider
        given = [lists[d] for d in chunk] + (lists[-1:] if teams - 1 in chunk else [])
        riders = [w_keep, w_send] if first else []
        held.append(
            call(
                functools.partial(
                    backward_kernel, chips, teams, slots, piece, chunk, len(riders)
                ),
                "backward",
                [*given, *backs, *riders],
                [any_space] * (len(given) + teams) + [vmem] * len(riders),
                [shaped(moved, part)] * 2,
                [
                    id_scratch(count)[0],
                    pltpu.VMEM((slab, part), bf16),
                    pltpu.VMEM((2 * rows, part), f32),
                    *id_scratch(count)[1:],
                    pltpu.SemaphoreType.DMA((count + teams,)),
                    pltpu.SemaphoreType.DMA,
                ],
                count * list_flops,
                rows * padded * 14 + count * list_bytes + slab * padded * 2 + 4 * MIB,
                after=[value[0] for value in held],
            )
        )
    mark = [held[1][0]]
    for chunk, (keep, send) in zip(chunks, held):
        moved = keep.shape[0]
        paired.append(
            call(
                functools.partial(pair_kernel, chips),
                "pair_sum",
                [keep, swap(send, "row", 1)],
                [vmem] * 2,
                [shaped(moved // chips, part)] * chips,
                [],
                moved * part,
                moved * padded * 6 + 3 * MIB,
                after=mark,
            )
        )
        mark = paired[0][:1]
    mark = paired[1][:1]
    for chunk, pieces in zip(chunks, paired):
        count = len(chunk)
        first = chunk is chunks[0]
        outs = [shaped(piece + first * rider, part)] * count + [shaped(rider, part)] * first
        sums = call(
            functools.partial(plane_kernel, chips, count),
            "plane_sum",
            plane_total(pieces),
            [vmem] * chips,
            outs,
            [],
            chips * count * piece * part,
            chips * (count * piece + rider) * padded * 4 + 3 * MIB,
            after=mark,
        )
        for d, value in zip(chunk, sums):
            slices[d] = swap(value, "team", d) if d else value
        mark = []
        if first:
            w_plane = sums[count]
    w_parts = [w_plane] + [
        slices[d] if d in chunks[0] else swap(w_plane, "team", d) for d in range(1, teams)
    ]
    (w_total,) = call(
        functools.partial(weight_total_kernel, teams),
        "weight_total",
        w_parts,
        [vmem] * teams,
        [shaped(rider, part)],
        [],
        half * width,
        6 * MIB,
        after=sums[:1],
    )
    (w_half,) = call(
        functools.partial(weight_half_kernel, chips, teams),
        "weight_half",
        plane_total([w_total] * chips),
        [vmem] * chips,
        [shaped(half, width)],
        [],
        half * width,
        6 * MIB,
        after=[slices[d] for d in chunks[1][1:]],
    )
    (grad_weight,) = call(
        functools.partial(whole_kernel, 1.0 / math.sqrt(nodes)),
        "weight_whole",
        [w_half, swap(w_half, "row", 1)],
        [vmem] * 2,
        [shaped(width, width, kind=f32)],
        [],
        half * width,
        6 * MIB,
    )
    (grad_features,) = call(
        functools.partial(join_kernel, teams),
        "join",
        slices,
        [vmem] * teams,
        [shaped(piece, width)],
        [pltpu.VMEM((teams, piece, part), bf16)],
        piece * width,
        teams * piece * padded * 8 + 3 * MIB,
    )

    return (output, grad_weight, grad_features[None])


def solution(mesh):
    placed = (
        P("row", None),
        P(),
        P(),
        P("row"),
        P("row"),
        P("row", "team", None, None, None),
        P("row", "team", None),
        P("row", "team", None),
        P("row", "team"),
    )
    return jax.shard_map(
        per_device,
        mesh=mesh,
        in_specs=placed,
        out_specs=(P(("row", "team"), None), P(), P("team", "row", None)),
        check_vma=False,
    )
```

```python
import functools
import math

import jax
import jax.numpy as jnp
from jax import lax
from jax.experimental import pallas as pl
from jax.experimental.pallas import tpu as pltpu
from jax.sharding import PartitionSpec as P

BLOCK = 128
GROUP = 4
ID_ROWS = 16
MIB = 1 << 20


def lanes(width):
    return -(-width // 128) * 128


def swap(value, axis, flip):
    size = lax.axis_size(axis)
    return lax.ppermute(value, axis, [(i, i ^ flip) for i in range(size)])


def load_ids(ids_vmem, ids_smem, lists, slots, sem, meanwhile):
    for d in range(lists.shape[0]):
        rows = lists[d, slots * BLOCK :, :].astype(jnp.float32)
        ids_vmem[d] = rows.astype(jnp.int32)[:8]
    copy = pltpu.make_async_copy(ids_vmem, ids_smem, sem)
    copy.start()
    meanwhile()
    copy.wait()


def each_group(ids, place, given, visit):
    for i, d in enumerate(given):
        live = ids[i, 2, 0]

        def step(group, carry, i=i, d=d, live=live):
            visit(i, place[0] ^ d, group * GROUP, live)
            return carry

        lax.fori_loop(0, (live + GROUP - 1) // GROUP, step, 0)


def fetch_late(place, teams, middle, relayed, target, sem):
    at_end = (place[0] == 0) | (place[0] == teams - 1)

    @pl.when(at_end)
    def _():
        pltpu.make_async_copy(relayed, target, sem).start()

    @pl.when(jnp.logical_not(at_end))
    def _():
        pltpu.make_async_copy(middle, target, sem).start()

    return pltpu.make_async_copy(middle, target, sem)


def forward_visit(panels, panel_rows, lists, ids, totals):
    def visit(i, panel, first, live):
        products = []
        for u in range(GROUP):
            slot = first + u
            start = panel * panel_rows + ids[i, 1, slot] * BLOCK
            source = panels[pl.ds(pl.multiple_of(start, BLOCK), BLOCK), :]
            block = lists[i, pl.ds(pl.multiple_of(slot * BLOCK, BLOCK), BLOCK), :]
            product = jnp.dot(block, source, preferred_element_type=jnp.float32)
            products.append(jnp.where(slot < live, product, 0.0))
        for u in range(GROUP):
            start = pl.multiple_of(ids[i, 0, first + u] * BLOCK, BLOCK)
            totals[pl.ds(start, BLOCK), :] += products[u]

    return visit


def prepare_kernel(slots, place, *refs):
    vals, row_ids, col_ids, count = refs[:4]
    rows, cols, lives, tail, sems = refs[-5:]
    mine = refs[4] if len(refs) == 10 else refs[5]
    blocks = slots * BLOCK
    moves = [(row_ids, rows), (col_ids, cols), (count, lives), (vals, mine.at[pl.ds(0, blocks), :])]
    if len(refs) > 10:
        features, near = refs[4], refs[6]
        width = near.shape[1]
        start = pl.multiple_of(place[0] * width, width)
        moves.append((features.at[:, pl.ds(start, width)], near))
    copies = [
        pltpu.make_async_copy(source, target, sems.at[i])
        for i, (source, target) in enumerate(moves)
    ]
    for copy in copies:
        copy.start()
    tail[...] = jnp.zeros_like(tail)
    for copy in copies[:3]:
        copy.wait()
    tail[0:1, 0:slots] = rows[...].astype(jnp.float32)
    tail[1:2, 0:slots] = cols[...].astype(jnp.float32)
    tail[2:3, 0:1] = lives[...].astype(jnp.float32)
    mine[pl.ds(blocks, ID_ROWS), :] = tail[...].astype(jnp.bfloat16)
    for copy in copies[3:]:
        copy.wait()


def early_kernel(chips, teams, slots, place, *refs):
    near = refs[:chips]
    far = refs[chips : 2 * chips]
    early = teams - 1
    given = refs[2 * chips : 2 * chips + early]
    weight, table = refs[2 * chips + early : 2 * chips + early + 2]
    totals, late_panel, *kept = refs[2 * chips + early + 2 : 2 * chips + early + 6]
    panels, lists, ids_vmem, ids_smem, sems, id_sem = refs[2 * chips + early + 6 :]
    slab = near[0].shape[0]
    panel_rows = panels.shape[0] // teams
    team, chip, core = place[0], place[1], place[2]
    copies = []
    for d in range(early):
        copies.append(pltpu.make_async_copy(given[d], lists.at[d], sems.at[d]))
    for d in range(chips):
        for side, source in ((core, near[d]), (1 - core, far[d])):
            start = pl.multiple_of((2 * (chip ^ d) + side) * slab, slab)
            target = panels.at[pl.ds(start, slab), :]
            copies.append(pltpu.make_async_copy(source, target, sems.at[len(copies)]))
    for source, target in zip((weight, table), kept):
        copies.append(pltpu.make_async_copy(source, target, sems.at[len(copies)]))
    for copy in copies:
        copy.start()

    def clear():
        totals[...] = jnp.zeros_like(totals)

    for copy in copies[:early]:
        copy.wait()
    load_ids(ids_vmem, ids_smem, lists, slots, id_sem, clear)
    for copy in copies[early:]:
        copy.wait()
    visit = forward_visit(panels, panel_rows, lists, ids_smem, totals)
    each_group(ids_smem, place, range(early), visit)
    start = pl.multiple_of((team ^ early) * panel_rows, panel_rows)
    late_panel[...] = panels[pl.ds(start, panel_rows), :]


def late_kernel(teams, slots, place, *refs):
    middle, relayed, begun, panel = refs[:4]
    outs = refs[4 : 4 + teams]
    totals, lists, ids_vmem, ids_smem, sem, id_sem = refs[4 + teams :]
    fetch = fetch_late(place, teams, middle, relayed, lists.at[0], sem)

    def take():
        totals[...] = begun[...]

    fetch.wait()
    load_ids(ids_vmem, ids_smem, lists, slots, id_sem, take)
    visit = forward_visit(panel, 0, lists, ids_smem, totals)
    each_group(ids_smem, place, [teams - 1], visit)
    share = outs[0].shape[0]
    for d in range(teams):
        start = pl.multiple_of((place[0] ^ d) * share, share)
        outs[d][...] = totals[pl.ds(start, share), :].astype(jnp.bfloat16)


def layer_kernel(teams, place, *refs):
    parts = refs[:teams]
    weight, table, *fixed = refs[teams : teams + 4]
    output, grad_pre = refs[teams + 4 : teams + 6]
    backs = refs[teams + 6 : 2 * teams + 6]
    labels, mask, sems = refs[2 * teams + 6 :]
    team = place[0]
    width = parts[0].shape[1]
    copies = [
        pltpu.make_async_copy(source, target, sems.at[i])
        for i, (source, target) in enumerate(zip(fixed, (labels, mask)))
    ]
    for copy in copies:
        copy.start()

    def weight_rows(d):
        return weight[pl.ds(pl.multiple_of((team ^ d) * width, width), width), :]

    preact = jnp.dot(parts[0][...], weight_rows(0), preferred_element_type=jnp.float32)
    for d in range(1, teams):
        preact += jnp.dot(parts[d][...], weight_rows(d), preferred_element_type=jnp.float32)
    sigma = 1.0 / (1.0 + jnp.exp(-preact))
    active = preact * sigma
    output[...] = active.astype(jnp.bfloat16)
    classes = table.shape[0]
    for copy in copies:
        copy.wait()
    row_labels = labels[pl.ds(team, 1), :]
    row_mask = mask[pl.ds(team, 1), :].astype(jnp.float32)
    rows = row_labels.shape[1]
    index = lax.broadcasted_iota(jnp.int32, (classes, rows), 0)
    known = jnp.where(index == row_labels, row_mask, 0.0).astype(jnp.bfloat16)
    held = jnp.broadcast_to(row_mask * (1.0 / 8.0), (8, rows)).astype(jnp.bfloat16)
    across = (((0,), (0,)), ((), ()))
    target = lax.dot_general(known, table[...], across, preferred_element_type=jnp.float32)
    ones = jnp.ones((8, table.shape[1]), jnp.bfloat16)
    masked = lax.dot_general(held, ones, across, preferred_element_type=jnp.float32)
    slope = sigma * (1.0 + preact * (1.0 - sigma))
    grad = ((masked * active - target) * slope).astype(jnp.bfloat16)
    grad_pre[...] = grad
    for d in range(teams):
        backs[d][...] = lax.dot_general(
            grad, weight_rows(d), (((1,), (1,)), ((), ())), preferred_element_type=jnp.float32
        ).astype(jnp.bfloat16)


def weight_kernel(teams, chips, place, *refs):
    parts = refs[:teams]
    grad_pre, keep, send, term = refs[teams:]
    width = parts[0].shape[1]
    for d in range(teams):
        start = pl.multiple_of((place[0] ^ d) * width, width)
        term[pl.ds(start, width), :] = lax.dot_general(
            parts[d][...], grad_pre[...], (((0,), (0,)), ((), ())), preferred_element_type=jnp.float32
        ).astype(jnp.bfloat16)
    half = term.shape[0] // 2
    rows = half // chips
    for out, side in ((keep, place[2]), (send, 1 - place[2])):
        for q in range(chips):
            held = pl.ds(pl.multiple_of(side * half + q * rows, rows), rows)
            for t in range(teams):
                start = (q * teams + t) * rows
                out[start : start + rows, :] = term[held, t * width : (t + 1) * width]


def tree(values):
    while len(values) > 1:
        values = [values[i] + values[i + 1] for i in range(0, len(values), 2)]
    return values[0]


def weight_total_kernel(teams, place, *refs):
    out = refs[teams]
    rows = out.shape[0]
    values = [ref[ref.shape[0] - rows :, :].astype(jnp.float32) for ref in refs[:teams]]
    out[...] = tree(values).astype(out.dtype)


def weight_half_kernel(chips, teams, place, *refs):
    out = refs[chips]
    rows = refs[0].shape[0] // teams
    width = refs[0].shape[1]
    for d in range(chips):
        held = pl.ds(pl.multiple_of((place[1] ^ d) * rows, rows), rows)
        for t in range(teams):
            out[held, t * width : (t + 1) * width] = refs[d][t * rows : (t + 1) * rows, :]


def whole_kernel(scale, place, mine, taken, out):
    rows = mine.shape[0]
    for value, here in ((mine, place[2]), (taken, 1 - place[2])):
        held = pl.ds(pl.multiple_of(here * rows, rows), rows)
        out[held, :] = value[...].astype(jnp.float32) * scale


def backward_kernel(chips, teams, slots, piece, chunk, riders, place, *refs):
    count = len(chunk)
    last = teams - 1 in chunk
    given = refs[: count + last]
    backs = refs[count + last : count + last + teams]
    refs = refs[count + last + teams :]
    at_end = (place[0] == 0) | (place[0] == teams - 1)

    def held(i, here):
        if last and i == count - 1:
            return jnp.where(at_end, given[i + 1][here, :], given[i][here, :])
        return given[i][here, :]

    rider_refs, refs = refs[:riders], refs[riders:]
    keep, send, rows, totals, ids_vmem, ids_smem, id_sem = refs
    team, core = place[0], place[2]
    share = backs[0].shape[0]
    per_piece = piece // BLOCK
    for i in range(count):
        tail = held(i, pl.ds(slots * BLOCK, ID_ROWS)).astype(jnp.float32)
        ids_vmem[i] = tail.astype(jnp.int32)[:8]
    copy = pltpu.make_async_copy(ids_vmem, ids_smem, id_sem)
    copy.start()
    totals[...] = jnp.zeros_like(totals)
    for d in range(teams):
        start = pl.multiple_of((team ^ d) * share, share)
        rows[pl.ds(start, share), :] = backs[d][...]
    copy.wait()

    def visit(i, panel, first, live):
        products = []
        for u in range(GROUP):
            slot = first + u
            start = pl.multiple_of(ids_smem[i, 0, slot] * BLOCK, BLOCK)
            source = rows[pl.ds(start, BLOCK), :]
            block = held(i, pl.ds(pl.multiple_of(slot * BLOCK, BLOCK), BLOCK))
            product = lax.dot_general(
                block, source, (((0,), (0,)), ((), ())), preferred_element_type=jnp.float32
            )
            products.append(jnp.where(slot < live, product, 0.0))
        for u in range(GROUP):
            col = ids_smem[i, 1, first + u]
            owner = col // per_piece
            slot_half = (owner % 2) ^ core
            slot_chip = owner // 2
            start = ((slot_half * chips + slot_chip) * count + i) * piece
            start = pl.multiple_of(start + (col % per_piece) * BLOCK, BLOCK)
            totals[pl.ds(start, BLOCK), :] += products[u]

    each_group(ids_smem, place, chunk, visit)
    size = count * piece
    step = keep.shape[0] // chips
    for side, out in enumerate((keep, send)):
        for q in range(chips):
            here = (side * chips + q) * size
            out[q * step : q * step + size, :] = totals[here : here + size, :].astype(jnp.bfloat16)
            if riders:
                more = step - size
                rider = rider_refs[side][q * more : (q + 1) * more, :]
                out[q * step + size : (q + 1) * step, :] = rider


def pair_kernel(chips, place, keep, taken, *outs):
    rows = outs[0].shape[0]
    for d in range(chips):
        here = pl.ds(pl.multiple_of((place[1] ^ d) * rows, rows), rows)
        total = keep[here, :].astype(jnp.float32) + taken[here, :].astype(jnp.float32)
        outs[d][...] = total.astype(jnp.bfloat16)


def plane_kernel(chips, count, place, *refs):
    parts, outs = refs[:chips], refs[chips:]
    rider = outs[count] if len(outs) > count else None
    rows = outs[0].shape[0] - (rider.shape[0] if rider is not None else 0)

    def total(here):
        value = parts[0][here, :].astype(jnp.float32)
        for part in parts[1:]:
            value += part[here, :].astype(jnp.float32)
        return value.astype(jnp.bfloat16)

    for i in range(count):
        outs[i][:rows, :] = total(slice(i * rows, (i + 1) * rows))
    if rider is not None:
        value = total(slice(count * rows, None))
        rider[...] = value
        for i in range(count):
            outs[i][rows:, :] = value


def join_kernel(teams, place, *refs):
    parts = refs[:teams]
    out, held = refs[teams:]
    width = parts[0].shape[1]
    for d in range(teams):
        held[place[0] ^ d] = parts[d][: held.shape[1], :]
    for d in range(teams):
        out[:, d * width : (d + 1) * width] = held[d]


def call(kernel, name, operands, spaces, out_shapes, scratch, flops, limit, after=()):
    moved = sum(math.prod(x.shape) * x.dtype.itemsize for x in (*operands, *out_shapes))
    specs = [pl.BlockSpec(memory_space=space) for space in spaces]
    specs += [pl.BlockSpec(memory_space=pl.ANY) for _ in after]
    given = len(operands)

    def body(*refs):
        row = lax.axis_index("row")
        place = (lax.axis_index("team"), row // 2, row % 2)
        kernel(place, *refs[:given], *refs[given + len(after) :])

    return pl.pallas_call(
        body,
        name=name,
        in_specs=specs,
        out_specs=[pl.BlockSpec(memory_space=pltpu.VMEM) for _ in out_shapes],
        out_shape=out_shapes,
        scratch_shapes=scratch,
        cost_estimate=pl.CostEstimate(
            flops=flops, bytes_accessed=moved if flops else 0, transcendentals=0
        ),
        compiler_params=pltpu.CompilerParams(vmem_limit_bytes=limit),
    )(*operands, *after)


def gather_lists(mine, teams, gate):
    if teams == 4:
        two = swap(mine, "team", 2)
        one = swap(mine, "team", 1)
        relayed = lax.ppermute(two, "team", [(2, 3), (1, 0)])
        held, _ = lax.optimization_barrier((mine, gate(two, one)))
        middle = lax.ppermute(held, "team", [(1, 2), (2, 1)])
        return [mine, one, two], [middle, relayed]
    early = [mine] + [swap(mine, "team", d) for d in range(1, teams - 1)]
    last = swap(mine, "team", teams - 1)
    return early, [last, last]


def per_device(
    features, weight, table, labels, label_mask, block_vals, block_row, block_col, block_count
):
    slab, width = features.shape
    slots = block_vals.shape[2]
    rows_n = lax.axis_size("row")
    teams = lax.axis_size("team")
    chips = rows_n // 2
    nodes = slab * rows_n
    panel_rows = nodes // teams
    part = width // teams
    share = slab // teams
    piece = panel_rows // rows_n
    team = lax.axis_index("team")
    bf16, f32 = jnp.bfloat16, jnp.float32
    any_space, vmem = pl.ANY, pltpu.VMEM
    padded = lanes(part)
    payload = slots * BLOCK + ID_ROWS

    def shaped(*dims, kind=bf16):
        return jax.ShapeDtypeStruct(dims, kind)

    def id_scratch(count):
        return [
            pltpu.VMEM((count, payload, BLOCK), bf16),
            pltpu.VMEM((count, 8, BLOCK), jnp.int32),
            pltpu.SMEM((count, 8, BLOCK), jnp.int32),
        ]

    list_bytes = payload * BLOCK * 2
    list_flops = 2 * slots * BLOCK * BLOCK * part

    aligned = part % 128 == 0
    prepared = call(
        functools.partial(prepare_kernel, slots),
        "prepare",
        [
            block_vals.reshape(slots * BLOCK, BLOCK),
            block_row.reshape(1, slots),
            block_col.reshape(1, slots),
            block_count,
            *([features] if aligned else []),
        ],
        [pltpu.HBM] * (4 + aligned),
        [shaped(payload, BLOCK)] + [shaped(slab, part)] * aligned,
        [
            pltpu.VMEM((1, slots), jnp.int32),
            pltpu.VMEM((1, slots), jnp.int32),
            pltpu.VMEM((1, 1), jnp.int32),
            pltpu.VMEM((ID_ROWS, BLOCK), f32),
            pltpu.SemaphoreType.DMA((5,)),
        ],
        0,
        60 * MIB,
    )
    mine = prepared[0]
    own = prepared[1] if aligned else lax.dynamic_slice_in_dim(features, team * part, part, 1)
    beside = swap(own, "row", 1)
    near = [own] + [swap(own, "row", 2 * d) for d in range(1, chips)]
    early, late = gather_lists(mine, teams, lambda two, one: one)
    far = [beside] + [swap(value, "row", 1) for value in near[1:]]

    ids = id_scratch(teams - 1)
    begun, late_panel, weight_here, table_here = call(
        functools.partial(early_kernel, chips, teams, slots),
        "early_products",
        [*near, *far, *early, weight, table],
        [any_space] * (2 * chips + teams + 1),
        [
            shaped(slab, part, kind=f32),
            shaped(panel_rows, part),
            shaped(*weight.shape),
            shaped(*table.shape),
        ],
        [
            pltpu.VMEM((nodes, part), bf16),
            *ids,
            pltpu.SemaphoreType.DMA((2 * chips + teams + 1,)),
            pltpu.SemaphoreType.DMA,
        ],
        0,
        (nodes + panel_rows) * padded * 2 + teams * list_bytes + slab * padded * 4 + 4 * MIB,
    )
    ids = id_scratch(1)
    sent = call(
        functools.partial(late_kernel, teams, slots),
        "late_products",
        [*late, begun, late_panel],
        [any_space, any_space, vmem, vmem],
        [shaped(share, part)] * teams,
        [
            pltpu.VMEM((slab, part), f32),
            *ids,
            pltpu.SemaphoreType.DMA,
            pltpu.SemaphoreType.DMA,
        ],
        list_flops,
        (panel_rows + 5 * slab) * padded * 2 + list_bytes + 3 * MIB,
    )
    aggs = [sent[0]] + [swap(sent[d], "team", d) for d in range(1, teams)]

    output, grad_pre, *backs = call(
        functools.partial(layer_kernel, teams),
        "layer",
        [
            *aggs,
            weight_here,
            table_here,
            labels.reshape(teams, share),
            label_mask.reshape(teams, share),
        ],
        [vmem] * (teams + 2) + [any_space] * 2,
        [shaped(share, width)] * 2 + [shaped(share, part)] * teams,
        [
            pltpu.VMEM((teams, share), jnp.int32),
            pltpu.VMEM((teams, share), jnp.int32),
            pltpu.SemaphoreType.DMA((2,)),
        ],
        4 * share * width * width,
        16 * MIB,
    )
    backs = [backs[0]] + [swap(backs[d], "team", d) for d in range(1, teams)]

    half = width // 2
    rider = half // chips * teams
    w_keep, w_send = call(
        functools.partial(weight_kernel, teams, chips),
        "weight_term",
        [*aggs, grad_pre],
        [vmem] * (teams + 1),
        [shaped(chips * rider, part)] * 2,
        [pltpu.VMEM((width, width), bf16)],
        2 * share * width * width,
        12 * MIB,
    )

    def plane_total(pieces):
        return [pieces[0]] + [swap(pieces[d], "row", 2 * d) for d in range(1, chips)]

    chunks = [list(range(teams // 2, teams)), list(range(teams // 2))]
    lists = early + late
    slices = [None] * teams
    held, paired = [], []
    for chunk in chunks:
        count = len(chunk)
        first = chunk is chunks[0]
        rows = chips * count * piece
        moved = rows + first * chips * rider
        given = [lists[d] for d in chunk] + (lists[-1:] if teams - 1 in chunk else [])
        riders = [w_keep, w_send] if first else []
        held.append(
            call(
                functools.partial(
                    backward_kernel, chips, teams, slots, piece, chunk, len(riders)
                ),
                "backward",
                [*given, *backs, *riders],
                [vmem] * (len(given) + teams + len(riders)),
                [shaped(moved, part)] * 2,
                [
                    pltpu.VMEM((slab, part), bf16),
                    pltpu.VMEM((2 * rows, part), f32),
                    *id_scratch(count)[1:],
                    pltpu.SemaphoreType.DMA,
                ],
                count * list_flops,
                rows * padded * 14 + (count + 1) * list_bytes + slab * padded * 4 + 4 * MIB,
                after=[value[0] for value in held],
            )
        )
    mark = [held[1][0]]
    for chunk, (keep, send) in zip(chunks, held):
        moved = keep.shape[0]
        paired.append(
            call(
                functools.partial(pair_kernel, chips),
                "pair_sum",
                [keep, swap(send, "row", 1)],
                [vmem] * 2,
                [shaped(moved // chips, part)] * chips,
                [],
                moved * part,
                moved * padded * 6 + 3 * MIB,
                after=mark,
            )
        )
        mark = paired[0][:1]
    mark = paired[1][:1]
    for chunk, pieces in zip(chunks, paired):
        count = len(chunk)
        first = chunk is chunks[0]
        outs = [shaped(piece + first * rider, part)] * count + [shaped(rider, part)] * first
        sums = call(
            functools.partial(plane_kernel, chips, count),
            "plane_sum",
            plane_total(pieces),
            [vmem] * chips,
            outs,
            [],
            chips * count * piece * part,
            chips * (count * piece + rider) * padded * 4 + 3 * MIB,
            after=mark,
        )
        for d, value in zip(chunk, sums):
            slices[d] = swap(value, "team", d) if d else value
        mark = []
        if first:
            w_plane = sums[count]
    w_parts = [w_plane] + [
        slices[d] if d in chunks[0] else swap(w_plane, "team", d) for d in range(1, teams)
    ]
    (w_total,) = call(
        functools.partial(weight_total_kernel, teams),
        "weight_total",
        w_parts,
        [vmem] * teams,
        [shaped(rider, part)],
        [],
        half * width,
        6 * MIB,
        after=sums[:1],
    )
    (w_half,) = call(
        functools.partial(weight_half_kernel, chips, teams),
        "weight_half",
        plane_total([w_total] * chips),
        [vmem] * chips,
        [shaped(half, width)],
        [],
        half * width,
        6 * MIB,
        after=[slices[d] for d in chunks[1][1:]],
    )
    (grad_weight,) = call(
        functools.partial(whole_kernel, 1.0 / math.sqrt(nodes)),
        "weight_whole",
        [w_half, swap(w_half, "row", 1)],
        [vmem] * 2,
        [shaped(width, width, kind=f32)],
        [],
        half * width,
        6 * MIB,
    )
    (grad_features,) = call(
        functools.partial(join_kernel, teams),
        "join",
        slices,
        [vmem] * teams,
        [shaped(piece, width)],
        [pltpu.VMEM((teams, piece, part), bf16)],
        piece * width,
        teams * piece * padded * 8 + 3 * MIB,
    )

    return (output, grad_weight, grad_features[None])


def solution(mesh):
    placed = (
        P("row", None),
        P(),
        P(),
        P("row"),
        P("row"),
        P("row", "team", None, None, None),
        P("row", "team", None),
        P("row", "team", None),
        P("row", "team"),
    )
    return jax.shard_map(
        per_device,
        mesh=mesh,
        in_specs=placed,
        out_specs=(P(("row", "team"), None), P(), P("team", "row", None)),
        check_vma=False,
    )
```

```python
import functools
import math

import jax
import jax.numpy as jnp
from jax import lax
from jax.experimental import pallas as pl
from jax.experimental.pallas import tpu as pltpu
from jax.sharding import PartitionSpec as P

BLOCK = 128
GROUP = 4
ID_ROWS = 16
MIB = 1 << 20


def lanes(width):
    return -(-width // 128) * 128


def swap(value, axis, flip):
    size = lax.axis_size(axis)
    return lax.ppermute(value, axis, [(i, i ^ flip) for i in range(size)])


def load_ids(ids_vmem, ids_smem, lists, slots, sem, meanwhile):
    for d in range(lists.shape[0]):
        rows = lists[d, slots * BLOCK :, :].astype(jnp.float32)
        ids_vmem[d] = rows.astype(jnp.int32)[:8]
    copy = pltpu.make_async_copy(ids_vmem, ids_smem, sem)
    copy.start()
    meanwhile()
    copy.wait()


def each_group(ids, place, given, visit):
    for i, d in enumerate(given):
        live = ids[i, 2, 0]

        def step(group, carry, i=i, d=d, live=live):
            visit(i, place[0] ^ d, group * GROUP, live)
            return carry

        lax.fori_loop(0, (live + GROUP - 1) // GROUP, step, 0)


def forward_visit(panels, panel_rows, lists, ids, totals):
    def visit(i, panel, first, live):
        products = []
        for u in range(GROUP):
            slot = first + u
            start = panel * panel_rows + ids[i, 1, slot] * BLOCK
            source = panels[pl.ds(pl.multiple_of(start, BLOCK), BLOCK), :]
            block = lists[i, pl.ds(pl.multiple_of(slot * BLOCK, BLOCK), BLOCK), :]
            product = jnp.dot(block, source, preferred_element_type=jnp.float32)
            products.append(jnp.where(slot < live, product, 0.0))
        for u in range(GROUP):
            start = pl.multiple_of(ids[i, 0, first + u] * BLOCK, BLOCK)
            totals[pl.ds(start, BLOCK), :] += products[u]

    return visit


def prepare_kernel(slots, place, *refs):
    vals, row_ids, col_ids, count = refs[:4]
    rows, cols, lives, tail, sems = refs[-5:]
    mine = refs[4] if len(refs) == 10 else refs[5]
    blocks = slots * BLOCK
    moves = [(row_ids, rows), (col_ids, cols), (count, lives), (vals, mine.at[pl.ds(0, blocks), :])]
    if len(refs) > 10:
        features, near = refs[4], refs[6]
        width = near.shape[1]
        start = pl.multiple_of(place[0] * width, width)
        moves.append((features.at[:, pl.ds(start, width)], near))
    copies = [
        pltpu.make_async_copy(source, target, sems.at[i])
        for i, (source, target) in enumerate(moves)
    ]
    for copy in copies:
        copy.start()
    tail[...] = jnp.zeros_like(tail)
    for copy in copies[:3]:
        copy.wait()
    tail[0:1, 0:slots] = rows[...].astype(jnp.float32)
    tail[1:2, 0:slots] = cols[...].astype(jnp.float32)
    tail[2:3, 0:1] = lives[...].astype(jnp.float32)
    mine[pl.ds(blocks, ID_ROWS), :] = tail[...].astype(jnp.bfloat16)
    for copy in copies[3:]:
        copy.wait()


def early_kernel(chips, teams, slots, place, *refs):
    near = refs[:chips]
    far = refs[chips : 2 * chips]
    early = teams - 1
    given = refs[2 * chips : 2 * chips + early]
    weight, table = refs[2 * chips + early : 2 * chips + early + 2]
    totals, late_panel, *kept = refs[2 * chips + early + 2 : 2 * chips + early + 6]
    panels, lists, ids_vmem, ids_smem, sems, id_sem = refs[2 * chips + early + 6 :]
    slab = near[0].shape[0]
    panel_rows = panels.shape[0] // teams
    team, chip, core = place[0], place[1], place[2]
    copies = []
    for d in range(early):
        copies.append(pltpu.make_async_copy(given[d], lists.at[d], sems.at[d]))
    for d in range(chips):
        for side, source in ((core, near[d]), (1 - core, far[d])):
            start = pl.multiple_of((2 * (chip ^ d) + side) * slab, slab)
            target = panels.at[pl.ds(start, slab), :]
            copies.append(pltpu.make_async_copy(source, target, sems.at[len(copies)]))
    for source, target in zip((weight, table), kept):
        copies.append(pltpu.make_async_copy(source, target, sems.at[len(copies)]))
    for copy in copies:
        copy.start()

    def clear():
        totals[...] = jnp.zeros_like(totals)

    for copy in copies[:early]:
        copy.wait()
    load_ids(ids_vmem, ids_smem, lists, slots, id_sem, clear)
    for copy in copies[early:]:
        copy.wait()
    visit = forward_visit(panels, panel_rows, lists, ids_smem, totals)
    each_group(ids_smem, place, range(early), visit)
    start = pl.multiple_of((team ^ early) * panel_rows, panel_rows)
    late_panel[...] = panels[pl.ds(start, panel_rows), :]


def pick(place, teams, middle, relayed, here):
    at_end = (place[0] == 0) | (place[0] == teams - 1)
    return jnp.where(at_end, relayed[here, :], middle[here, :])


def late_kernel(teams, slots, place, *refs):
    middle, relayed, begun, panel = refs[:4]
    outs = refs[4 : 4 + teams]
    totals, lists, ids_vmem, ids_smem, id_sem = refs[4 + teams :]
    tail = pick(place, teams, middle, relayed, pl.ds(slots * BLOCK, ID_ROWS))
    ids_vmem[0] = tail.astype(jnp.float32).astype(jnp.int32)[:8]
    copy = pltpu.make_async_copy(ids_vmem, ids_smem, id_sem)
    copy.start()
    totals[...] = begun[...]
    lists[0] = pick(place, teams, middle, relayed, slice(None))
    copy.wait()
    visit = forward_visit(panel, 0, lists, ids_smem, totals)
    each_group(ids_smem, place, [teams - 1], visit)
    share = outs[0].shape[0]
    for d in range(teams):
        start = pl.multiple_of((place[0] ^ d) * share, share)
        outs[d][...] = totals[pl.ds(start, share), :].astype(jnp.bfloat16)


def layer_kernel(teams, place, *refs):
    parts = refs[:teams]
    weight, table, *fixed = refs[teams : teams + 4]
    output, grad_pre = refs[teams + 4 : teams + 6]
    backs = refs[teams + 6 : 2 * teams + 6]
    labels, mask, cols, sems = refs[2 * teams + 6 :]
    team = place[0]
    width = parts[0].shape[1]
    copies = [
        pltpu.make_async_copy(source, target, sems.at[i])
        for i, (source, target) in enumerate(zip(fixed, (labels, mask)))
    ]
    for copy in copies:
        copy.start()

    for d in range(teams):
        cols[team ^ d] = parts[d][...]
    agg = jnp.concatenate([cols[t] for t in range(teams)], axis=1)
    preact = jnp.dot(agg, weight[...], preferred_element_type=jnp.float32)
    sigma = 1.0 / (1.0 + jnp.exp(-preact))
    active = preact * sigma
    output[...] = active.astype(jnp.bfloat16)
    classes = table.shape[0]
    for copy in copies:
        copy.wait()
    row_labels = labels[pl.ds(team, 1), :]
    row_mask = mask[pl.ds(team, 1), :].astype(jnp.float32)
    rows = row_labels.shape[1]
    index = lax.broadcasted_iota(jnp.int32, (classes, rows), 0)
    known = jnp.where(index == row_labels, row_mask, 0.0).astype(jnp.bfloat16)
    held = jnp.broadcast_to(row_mask * (1.0 / 8.0), (8, rows)).astype(jnp.bfloat16)
    across = (((0,), (0,)), ((), ()))
    target = lax.dot_general(known, table[...], across, preferred_element_type=jnp.float32)
    ones = jnp.ones((8, table.shape[1]), jnp.bfloat16)
    masked = lax.dot_general(held, ones, across, preferred_element_type=jnp.float32)
    slope = sigma * (1.0 + preact * (1.0 - sigma))
    grad = ((masked * active - target) * slope).astype(jnp.bfloat16)
    grad_pre[...] = grad
    back = lax.dot_general(
        grad, weight[...], (((1,), (1,)), ((), ())), preferred_element_type=jnp.float32
    ).astype(jnp.bfloat16)
    for t in range(teams):
        cols[t] = back[:, t * width : (t + 1) * width]
    for d in range(teams):
        backs[d][...] = cols[team ^ d]


def weight_kernel(teams, chips, place, *refs):
    parts = refs[:teams]
    grad_pre, keep, send, term = refs[teams:]
    width = parts[0].shape[1]
    for d in range(teams):
        start = pl.multiple_of((place[0] ^ d) * width, width)
        term[pl.ds(start, width), :] = lax.dot_general(
            parts[d][...], grad_pre[...], (((0,), (0,)), ((), ())), preferred_element_type=jnp.float32
        ).astype(jnp.bfloat16)
    half = term.shape[0] // 2
    rows = half // chips
    for out, side in ((keep, place[2]), (send, 1 - place[2])):
        for q in range(chips):
            held = pl.ds(pl.multiple_of(side * half + q * rows, rows), rows)
            for t in range(teams):
                start = (q * teams + t) * rows
                out[start : start + rows, :] = term[held, t * width : (t + 1) * width]


def tree(values):
    while len(values) > 1:
        values = [values[i] + values[i + 1] for i in range(0, len(values), 2)]
    return values[0]


def weight_total_kernel(teams, place, *refs):
    out = refs[teams]
    rows = out.shape[0]
    values = [ref[ref.shape[0] - rows :, :].astype(jnp.float32) for ref in refs[:teams]]
    out[...] = tree(values).astype(out.dtype)


def weight_half_kernel(chips, teams, place, *refs):
    out = refs[chips]
    rows = refs[0].shape[0] // teams
    width = refs[0].shape[1]
    for d in range(chips):
        held = pl.ds(pl.multiple_of((place[1] ^ d) * rows, rows), rows)
        for t in range(teams):
            out[held, t * width : (t + 1) * width] = refs[d][t * rows : (t + 1) * rows, :]


def whole_kernel(scale, place, mine, taken, out):
    rows = mine.shape[0]
    for value, here in ((mine, place[2]), (taken, 1 - place[2])):
        held = pl.ds(pl.multiple_of(here * rows, rows), rows)
        out[held, :] = value[...].astype(jnp.float32) * scale


def backward_kernel(chips, teams, slots, piece, chunk, riders, place, *refs):
    count = len(chunk)
    last = teams - 1 in chunk
    given = refs[: count + last]
    backs = refs[count + last : count + last + teams]
    refs = refs[count + last + teams :]

    def held(i, here):
        if last and i == count - 1:
            return pick(place, teams, given[i], given[i + 1], here)
        return given[i][here, :]

    rider_refs, refs = refs[:riders], refs[riders:]
    keep, send, rows, totals, ids_vmem, ids_smem, id_sem = refs
    team, core = place[0], place[2]
    share = backs[0].shape[0]
    per_piece = piece // BLOCK
    for i in range(count):
        tail = held(i, pl.ds(slots * BLOCK, ID_ROWS)).astype(jnp.float32)
        ids_vmem[i] = tail.astype(jnp.int32)[:8]
    copy = pltpu.make_async_copy(ids_vmem, ids_smem, id_sem)
    copy.start()
    totals[...] = jnp.zeros_like(totals)
    for d in range(teams):
        start = pl.multiple_of((team ^ d) * share, share)
        rows[pl.ds(start, share), :] = backs[d][...]
    copy.wait()

    def visit(i, panel, first, live):
        products = []
        for u in range(GROUP):
            slot = first + u
            start = pl.multiple_of(ids_smem[i, 0, slot] * BLOCK, BLOCK)
            source = rows[pl.ds(start, BLOCK), :]
            block = held(i, pl.ds(pl.multiple_of(slot * BLOCK, BLOCK), BLOCK))
            product = lax.dot_general(
                block, source, (((0,), (0,)), ((), ())), preferred_element_type=jnp.float32
            )
            products.append(jnp.where(slot < live, product, 0.0))
        for u in range(GROUP):
            col = ids_smem[i, 1, first + u]
            owner = col // per_piece
            slot_half = (owner % 2) ^ core
            slot_chip = owner // 2
            start = ((slot_half * chips + slot_chip) * count + i) * piece
            start = pl.multiple_of(start + (col % per_piece) * BLOCK, BLOCK)
            totals[pl.ds(start, BLOCK), :] += products[u]

    each_group(ids_smem, place, chunk, visit)
    size = count * piece
    step = keep.shape[0] // chips
    for side, out in enumerate((keep, send)):
        for q in range(chips):
            here = (side * chips + q) * size
            out[q * step : q * step + size, :] = totals[here : here + size, :].astype(jnp.bfloat16)
            if riders:
                more = step - size
                rider = rider_refs[side][q * more : (q + 1) * more, :]
                out[q * step + size : (q + 1) * step, :] = rider


def pair_kernel(chips, place, keep, taken, *outs):
    rows = outs[0].shape[0]
    for d in range(chips):
        here = pl.ds(pl.multiple_of((place[1] ^ d) * rows, rows), rows)
        total = keep[here, :].astype(jnp.float32) + taken[here, :].astype(jnp.float32)
        outs[d][...] = total.astype(jnp.bfloat16)


def plane_kernel(chips, count, place, *refs):
    parts, outs = refs[:chips], refs[chips:]
    rider = outs[count] if len(outs) > count else None
    rows = outs[0].shape[0] - (rider.shape[0] if rider is not None else 0)

    def total(here):
        value = parts[0][here, :].astype(jnp.float32)
        for part in parts[1:]:
            value += part[here, :].astype(jnp.float32)
        return value.astype(jnp.bfloat16)

    for i in range(count):
        outs[i][:rows, :] = total(slice(i * rows, (i + 1) * rows))
    if rider is not None:
        value = total(slice(count * rows, None))
        rider[...] = value
        for i in range(count):
            outs[i][rows:, :] = value


def join_kernel(teams, place, *refs):
    parts = refs[:teams]
    out, held = refs[teams:]
    width = parts[0].shape[1]
    for d in range(teams):
        held[place[0] ^ d] = parts[d][: held.shape[1], :]
    for d in range(teams):
        out[:, d * width : (d + 1) * width] = held[d]


def call(kernel, name, operands, spaces, out_shapes, scratch, flops, limit, after=()):
    moved = sum(math.prod(x.shape) * x.dtype.itemsize for x in (*operands, *out_shapes))
    specs = [pl.BlockSpec(memory_space=space) for space in spaces]
    specs += [pl.BlockSpec(memory_space=pl.ANY) for _ in after]
    given = len(operands)

    def body(*refs):
        row = lax.axis_index("row")
        place = (lax.axis_index("team"), row // 2, row % 2)
        kernel(place, *refs[:given], *refs[given + len(after) :])

    return pl.pallas_call(
        body,
        name=name,
        in_specs=specs,
        out_specs=[pl.BlockSpec(memory_space=pltpu.VMEM) for _ in out_shapes],
        out_shape=out_shapes,
        scratch_shapes=scratch,
        cost_estimate=pl.CostEstimate(
            flops=flops, bytes_accessed=moved if flops else 0, transcendentals=0
        ),
        compiler_params=pltpu.CompilerParams(vmem_limit_bytes=limit),
    )(*operands, *after)


def gather_lists(mine, teams, gate):
    if teams == 4:
        two = swap(mine, "team", 2)
        one = swap(mine, "team", 1)
        relayed = lax.ppermute(two, "team", [(2, 3), (1, 0)])
        held, _ = lax.optimization_barrier((mine, gate(two, one)))
        middle = lax.ppermute(held, "team", [(1, 2), (2, 1)])
        return [mine, one, two], [middle, relayed]
    early = [mine] + [swap(mine, "team", d) for d in range(1, teams - 1)]
    last = swap(mine, "team", teams - 1)
    return early, [last, last]


def per_device(
    features, weight, table, labels, label_mask, block_vals, block_row, block_col, block_count
):
    slab, width = features.shape
    slots = block_vals.shape[2]
    rows_n = lax.axis_size("row")
    teams = lax.axis_size("team")
    chips = rows_n // 2
    nodes = slab * rows_n
    panel_rows = nodes // teams
    part = width // teams
    share = slab // teams
    piece = panel_rows // rows_n
    team = lax.axis_index("team")
    bf16, f32 = jnp.bfloat16, jnp.float32
    any_space, vmem = pl.ANY, pltpu.VMEM
    padded = lanes(part)
    payload = slots * BLOCK + ID_ROWS

    def shaped(*dims, kind=bf16):
        return jax.ShapeDtypeStruct(dims, kind)

    def id_scratch(count):
        return [
            pltpu.VMEM((count, payload, BLOCK), bf16),
            pltpu.VMEM((count, 8, BLOCK), jnp.int32),
            pltpu.SMEM((count, 8, BLOCK), jnp.int32),
        ]

    list_bytes = payload * BLOCK * 2
    list_flops = 2 * slots * BLOCK * BLOCK * part

    aligned = part % 128 == 0
    prepared = call(
        functools.partial(prepare_kernel, slots),
        "prepare",
        [
            block_vals.reshape(slots * BLOCK, BLOCK),
            block_row.reshape(1, slots),
            block_col.reshape(1, slots),
            block_count,
            *([features] if aligned else []),
        ],
        [pltpu.HBM] * (4 + aligned),
        [shaped(payload, BLOCK)] + [shaped(slab, part)] * aligned,
        [
            pltpu.VMEM((1, slots), jnp.int32),
            pltpu.VMEM((1, slots), jnp.int32),
            pltpu.VMEM((1, 1), jnp.int32),
            pltpu.VMEM((ID_ROWS, BLOCK), f32),
            pltpu.SemaphoreType.DMA((5,)),
        ],
        0,
        60 * MIB,
    )
    mine = prepared[0]
    own = prepared[1] if aligned else lax.dynamic_slice_in_dim(features, team * part, part, 1)
    beside = swap(own, "row", 1)
    near = [own] + [swap(own, "row", 2 * d) for d in range(1, chips)]
    early, late = gather_lists(mine, teams, lambda two, one: one)
    far = [beside] + [swap(value, "row", 1) for value in near[1:]]

    ids = id_scratch(teams - 1)
    begun, late_panel, weight_here, table_here = call(
        functools.partial(early_kernel, chips, teams, slots),
        "early_products",
        [*near, *far, *early, weight, table],
        [any_space] * (2 * chips + teams + 1),
        [
            shaped(slab, part, kind=f32),
            shaped(panel_rows, part),
            shaped(*weight.shape),
            shaped(*table.shape),
        ],
        [
            pltpu.VMEM((nodes, part), bf16),
            *ids,
            pltpu.SemaphoreType.DMA((2 * chips + teams + 1,)),
            pltpu.SemaphoreType.DMA,
        ],
        0,
        (nodes + panel_rows) * padded * 2 + teams * list_bytes + slab * padded * 4 + 4 * MIB,
    )
    ids = id_scratch(1)
    sent = call(
        functools.partial(late_kernel, teams, slots),
        "late_products",
        [*late, begun, late_panel],
        [vmem] * 4,
        [shaped(share, part)] * teams,
        [
            pltpu.VMEM((slab, part), f32),
            *ids,
            pltpu.SemaphoreType.DMA,
        ],
        list_flops,
        (panel_rows + 5 * slab) * padded * 2 + 3 * list_bytes + 3 * MIB,
    )
    aggs = [sent[0]] + [swap(sent[d], "team", d) for d in range(1, teams)]

    output, grad_pre, *backs = call(
        functools.partial(layer_kernel, teams),
        "layer",
        [
            *aggs,
            weight_here,
            table_here,
            labels.reshape(teams, share),
            label_mask.reshape(teams, share),
        ],
        [vmem] * (teams + 2) + [any_space] * 2,
        [shaped(share, width)] * 2 + [shaped(share, part)] * teams,
        [
            pltpu.VMEM((teams, share), jnp.int32),
            pltpu.VMEM((teams, share), jnp.int32),
            pltpu.VMEM((teams, share, part), bf16),
            pltpu.SemaphoreType.DMA((2,)),
        ],
        4 * share * width * width,
        16 * MIB,
    )
    backs = [backs[0]] + [swap(backs[d], "team", d) for d in range(1, teams)]

    half = width // 2
    rider = half // chips * teams
    w_keep, w_send = call(
        functools.partial(weight_kernel, teams, chips),
        "weight_term",
        [*aggs, grad_pre],
        [vmem] * (teams + 1),
        [shaped(chips * rider, part)] * 2,
        [pltpu.VMEM((width, width), bf16)],
        2 * share * width * width,
        12 * MIB,
    )

    def plane_total(pieces):
        return [pieces[0]] + [swap(pieces[d], "row", 2 * d) for d in range(1, chips)]

    chunks = [list(range(teams // 2, teams)), list(range(teams // 2))]
    lists = early + late
    slices = [None] * teams
    held, paired = [], []
    for chunk in chunks:
        count = len(chunk)
        first = chunk is chunks[0]
        rows = chips * count * piece
        moved = rows + first * chips * rider
        given = [lists[d] for d in chunk] + (lists[-1:] if teams - 1 in chunk else [])
        riders = [w_keep, w_send] if first else []
        held.append(
            call(
                functools.partial(
                    backward_kernel, chips, teams, slots, piece, chunk, len(riders)
                ),
                "backward",
                [*given, *backs, *riders],
                [vmem] * (len(given) + teams + len(riders)),
                [shaped(moved, part)] * 2,
                [
                    pltpu.VMEM((slab, part), bf16),
                    pltpu.VMEM((2 * rows, part), f32),
                    *id_scratch(count)[1:],
                    pltpu.SemaphoreType.DMA,
                ],
                count * list_flops,
                rows * padded * 14 + (count + 1) * list_bytes + slab * padded * 4 + 4 * MIB,
                after=[value[0] for value in held],
            )
        )
    mark = [held[1][0]]
    for chunk, (keep, send) in zip(chunks, held):
        moved = keep.shape[0]
        paired.append(
            call(
                functools.partial(pair_kernel, chips),
                "pair_sum",
                [keep, swap(send, "row", 1)],
                [vmem] * 2,
                [shaped(moved // chips, part)] * chips,
                [],
                moved * part,
                moved * padded * 6 + 3 * MIB,
                after=mark,
            )
        )
        mark = paired[0][:1]
    mark = paired[1][:1]
    for chunk, pieces in zip(chunks, paired):
        count = len(chunk)
        first = chunk is chunks[0]
        outs = [shaped(piece + first * rider, part)] * count + [shaped(rider, part)] * first
        sums = call(
            functools.partial(plane_kernel, chips, count),
            "plane_sum",
            plane_total(pieces),
            [vmem] * chips,
            outs,
            [],
            chips * count * piece * part,
            chips * (count * piece + rider) * padded * 4 + 3 * MIB,
            after=mark,
        )
        for d, value in zip(chunk, sums):
            slices[d] = swap(value, "team", d) if d else value
        mark = []
        if first:
            w_plane = sums[count]
    w_parts = [w_plane] + [
        slices[d] if d in chunks[0] else swap(w_plane, "team", d) for d in range(1, teams)
    ]
    (w_total,) = call(
        functools.partial(weight_total_kernel, teams),
        "weight_total",
        w_parts,
        [vmem] * teams,
        [shaped(rider, part)],
        [],
        half * width,
        6 * MIB,
        after=sums[:1],
    )
    (w_half,) = call(
        functools.partial(weight_half_kernel, chips, teams),
        "weight_half",
        plane_total([w_total] * chips),
        [vmem] * chips,
        [shaped(half, width)],
        [],
        half * width,
        6 * MIB,
        after=[slices[d] for d in chunks[1][1:]],
    )
    (grad_weight,) = call(
        functools.partial(whole_kernel, 1.0 / math.sqrt(nodes)),
        "weight_whole",
        [w_half, swap(w_half, "row", 1)],
        [vmem] * 2,
        [shaped(width, width, kind=f32)],
        [],
        half * width,
        6 * MIB,
    )
    (grad_features,) = call(
        functools.partial(join_kernel, teams),
        "join",
        slices,
        [vmem] * teams,
        [shaped(piece, width)],
        [pltpu.VMEM((teams, piece, part), bf16)],
        piece * width,
        teams * piece * padded * 8 + 3 * MIB,
    )

    return (output, grad_weight, grad_features[None])


def solution(mesh):
    placed = (
        P("row", None),
        P(),
        P(),
        P("row"),
        P("row"),
        P("row", "team", None, None, None),
        P("row", "team", None),
        P("row", "team", None),
        P("row", "team"),
    )
    return jax.shard_map(
        per_device,
        mesh=mesh,
        in_specs=placed,
        out_specs=(P(("row", "team"), None), P(), P("team", "row", None)),
        check_vma=False,
    )
```

```python
import functools
import math

import jax
import jax.numpy as jnp
from jax import lax
from jax.experimental import pallas as pl
from jax.experimental.pallas import tpu as pltpu
from jax.sharding import PartitionSpec as P

BLOCK = 128
GROUP = 4
ID_ROWS = 16
MIB = 1 << 20


def lanes(width):
    return -(-width // 128) * 128


def swap(value, axis, flip):
    size = lax.axis_size(axis)
    return lax.ppermute(value, axis, [(i, i ^ flip) for i in range(size)])


def load_ids(ids_vmem, ids_smem, lists, slots, sem, meanwhile):
    for d in range(lists.shape[0]):
        rows = lists[d, slots * BLOCK :, :].astype(jnp.float32)
        ids_vmem[d] = rows.astype(jnp.int32)[:8]
    copy = pltpu.make_async_copy(ids_vmem, ids_smem, sem)
    copy.start()
    meanwhile()
    copy.wait()


def each_group(ids, place, given, visit):
    for i, d in enumerate(given):
        live = ids[i, 2, 0]

        def step(group, carry, i=i, d=d, live=live):
            visit(i, place[0] ^ d, group * GROUP, live)
            return carry

        lax.fori_loop(0, (live + GROUP - 1) // GROUP, step, 0)


def forward_visit(panels, panel_rows, lists, ids, totals):
    def visit(i, panel, first, live):
        products = []
        for u in range(GROUP):
            slot = first + u
            start = panel * panel_rows + ids[i, 1, slot] * BLOCK
            source = panels[pl.ds(pl.multiple_of(start, BLOCK), BLOCK), :]
            block = lists[i, pl.ds(pl.multiple_of(slot * BLOCK, BLOCK), BLOCK), :]
            product = jnp.dot(block, source, preferred_element_type=jnp.float32)
            products.append(jnp.where(slot < live, product, 0.0))
        for u in range(GROUP):
            start = pl.multiple_of(ids[i, 0, first + u] * BLOCK, BLOCK)
            totals[pl.ds(start, BLOCK), :] += products[u]

    return visit


def prepare_kernel(slots, place, *refs):
    vals, row_ids, col_ids, count = refs[:4]
    rows, cols, lives, tail, sems = refs[-5:]
    mine = refs[4] if len(refs) == 10 else refs[5]
    blocks = slots * BLOCK
    moves = [(row_ids, rows), (col_ids, cols), (count, lives), (vals, mine.at[pl.ds(0, blocks), :])]
    if len(refs) > 10:
        features, near = refs[4], refs[6]
        width = near.shape[1]
        start = pl.multiple_of(place[0] * width, width)
        moves.append((features.at[:, pl.ds(start, width)], near))
    copies = [
        pltpu.make_async_copy(source, target, sems.at[i])
        for i, (source, target) in enumerate(moves)
    ]
    for copy in copies:
        copy.start()
    tail[...] = jnp.zeros_like(tail)
    for copy in copies[:3]:
        copy.wait()
    tail[0:1, 0:slots] = rows[...].astype(jnp.float32)
    tail[1:2, 0:slots] = cols[...].astype(jnp.float32)
    tail[2:3, 0:1] = lives[...].astype(jnp.float32)
    mine[pl.ds(blocks, ID_ROWS), :] = tail[...].astype(jnp.bfloat16)
    for copy in copies[3:]:
        copy.wait()


def early_kernel(chips, teams, slots, place, *refs):
    near = refs[:chips]
    far = refs[chips : 2 * chips]
    early = teams - 1
    given = refs[2 * chips : 2 * chips + early]
    weight, table = refs[2 * chips + early : 2 * chips + early + 2]
    totals, late_panel, *kept = refs[2 * chips + early + 2 : 2 * chips + early + 6]
    panels, lists, ids_vmem, ids_smem, sems, id_sem = refs[2 * chips + early + 6 :]
    slab = near[0].shape[0]
    panel_rows = panels.shape[0] // teams
    team, chip, core = place[0], place[1], place[2]
    copies = []
    for d in range(early):
        copies.append(pltpu.make_async_copy(given[d], lists.at[d], sems.at[d]))
    for d in range(chips):
        for side, source in ((core, near[d]), (1 - core, far[d])):
            start = pl.multiple_of((2 * (chip ^ d) + side) * slab, slab)
            target = panels.at[pl.ds(start, slab), :]
            copies.append(pltpu.make_async_copy(source, target, sems.at[len(copies)]))
    for source, target in zip((weight, table), kept):
        copies.append(pltpu.make_async_copy(source, target, sems.at[len(copies)]))
    for copy in copies:
        copy.start()

    def clear():
        totals[...] = jnp.zeros_like(totals)

    for copy in copies[:early]:
        copy.wait()
    load_ids(ids_vmem, ids_smem, lists, slots, id_sem, clear)
    for copy in copies[early:]:
        copy.wait()
    visit = forward_visit(panels, panel_rows, lists, ids_smem, totals)
    each_group(ids_smem, place, range(early), visit)
    start = pl.multiple_of((team ^ early) * panel_rows, panel_rows)
    late_panel[...] = panels[pl.ds(start, panel_rows), :]


def pick(place, teams, middle, relayed, here):
    at_end = (place[0] == 0) | (place[0] == teams - 1)
    return jnp.where(at_end, relayed[here, :], middle[here, :])


def late_kernel(teams, slots, place, *refs):
    middle, relayed, begun, panel = refs[:4]
    outs = refs[4 : 4 + teams]
    totals, lists, ids_vmem, ids_smem, id_sem = refs[4 + teams :]
    tail = pick(place, teams, middle, relayed, pl.ds(slots * BLOCK, ID_ROWS))
    ids_vmem[0] = tail.astype(jnp.float32).astype(jnp.int32)[:8]
    copy = pltpu.make_async_copy(ids_vmem, ids_smem, id_sem)
    copy.start()
    totals[...] = begun[...]
    lists[0] = pick(place, teams, middle, relayed, slice(None))
    copy.wait()
    visit = forward_visit(panel, 0, lists, ids_smem, totals)
    each_group(ids_smem, place, [teams - 1], visit)
    share = outs[0].shape[0]
    for d in range(teams):
        start = pl.multiple_of((place[0] ^ d) * share, share)
        outs[d][...] = totals[pl.ds(start, share), :].astype(jnp.bfloat16)


def layer_kernel(teams, place, *refs):
    parts = refs[:teams]
    weight, table, *fixed = refs[teams : teams + 4]
    output, grad_pre = refs[teams + 4 : teams + 6]
    backs = refs[teams + 6 : 2 * teams + 6]
    labels, mask, cols, sems = refs[2 * teams + 6 :]
    team = place[0]
    width = parts[0].shape[1]
    copies = [
        pltpu.make_async_copy(source, target, sems.at[i])
        for i, (source, target) in enumerate(zip(fixed, (labels, mask)))
    ]
    for copy in copies:
        copy.start()

    for d in range(teams):
        cols[team ^ d] = parts[d][...]
    agg = jnp.concatenate([cols[t] for t in range(teams)], axis=1)
    preact = jnp.dot(agg, weight[...], preferred_element_type=jnp.float32)
    sigma = 1.0 / (1.0 + jnp.exp(-preact))
    active = preact * sigma
    output[...] = active.astype(jnp.bfloat16)
    classes = table.shape[0]
    for copy in copies:
        copy.wait()
    row_labels = labels[pl.ds(team, 1), :]
    row_mask = mask[pl.ds(team, 1), :].astype(jnp.float32)
    rows = row_labels.shape[1]
    index = lax.broadcasted_iota(jnp.int32, (classes, rows), 0)
    known = jnp.where(index == row_labels, row_mask, 0.0).astype(jnp.bfloat16)
    held = jnp.broadcast_to(row_mask * (1.0 / 8.0), (8, rows)).astype(jnp.bfloat16)
    across = (((0,), (0,)), ((), ()))
    target = lax.dot_general(known, table[...], across, preferred_element_type=jnp.float32)
    ones = jnp.ones((8, table.shape[1]), jnp.bfloat16)
    masked = lax.dot_general(held, ones, across, preferred_element_type=jnp.float32)
    slope = sigma * (1.0 + preact * (1.0 - sigma))
    grad = ((masked * active - target) * slope).astype(jnp.bfloat16)
    grad_pre[...] = grad
    back = lax.dot_general(
        grad, weight[...], (((1,), (1,)), ((), ())), preferred_element_type=jnp.float32
    ).astype(jnp.bfloat16)
    for t in range(teams):
        cols[t] = back[:, t * width : (t + 1) * width]
    for d in range(teams):
        backs[d][...] = cols[team ^ d]


def weight_kernel(teams, chips, place, *refs):
    parts = refs[:teams]
    grad_pre, keep, send, term = refs[teams:]
    width = parts[0].shape[1]
    for d in range(teams):
        start = pl.multiple_of((place[0] ^ d) * width, width)
        term[pl.ds(start, width), :] = lax.dot_general(
            parts[d][...], grad_pre[...], (((0,), (0,)), ((), ())), preferred_element_type=jnp.float32
        ).astype(jnp.bfloat16)
    half = term.shape[0] // 2
    rows = half // chips
    for out, side in ((keep, place[2]), (send, 1 - place[2])):
        for q in range(chips):
            held = pl.ds(pl.multiple_of(side * half + q * rows, rows), rows)
            for t in range(teams):
                start = (q * teams + t) * rows
                out[start : start + rows, :] = term[held, t * width : (t + 1) * width]


def tree(values):
    while len(values) > 1:
        values = [values[i] + values[i + 1] for i in range(0, len(values), 2)]
    return values[0]


def weight_total_kernel(teams, place, *refs):
    out = refs[teams]
    rows = out.shape[0]
    values = [ref[ref.shape[0] - rows :, :].astype(jnp.float32) for ref in refs[:teams]]
    out[...] = tree(values).astype(out.dtype)


def whole_kernel(chips, teams, scale, place, *refs):
    out = refs[2 * chips]
    rows = refs[0].shape[0] // teams
    width = refs[0].shape[1]
    for side, pieces in ((place[2], refs[:chips]), (1 - place[2], refs[chips : 2 * chips])):
        for d in range(chips):
            start = (side * chips + (place[1] ^ d)) * rows
            held = pl.ds(pl.multiple_of(start, rows), rows)
            for t in range(teams):
                value = pieces[d][t * rows : (t + 1) * rows, :].astype(jnp.float32)
                out[held, t * width : (t + 1) * width] = value * scale


def backward_kernel(chips, teams, slots, piece, chunk, riders, place, *refs):
    count = len(chunk)
    last = teams - 1 in chunk
    given = refs[: count + last]
    backs = refs[count + last : count + last + teams]
    refs = refs[count + last + teams :]

    def held(i, here):
        if last and i == count - 1:
            return pick(place, teams, given[i], given[i + 1], here)
        return given[i][here, :]

    rider_refs, refs = refs[:riders], refs[riders:]
    keep, send, rows, totals, ids_vmem, ids_smem, id_sem = refs
    team, core = place[0], place[2]
    share = backs[0].shape[0]
    per_piece = piece // BLOCK
    for i in range(count):
        tail = held(i, pl.ds(slots * BLOCK, ID_ROWS)).astype(jnp.float32)
        ids_vmem[i] = tail.astype(jnp.int32)[:8]
    copy = pltpu.make_async_copy(ids_vmem, ids_smem, id_sem)
    copy.start()
    totals[...] = jnp.zeros_like(totals)
    for d in range(teams):
        start = pl.multiple_of((team ^ d) * share, share)
        rows[pl.ds(start, share), :] = backs[d][...]
    copy.wait()

    def visit(i, panel, first, live):
        products = []
        for u in range(GROUP):
            slot = first + u
            start = pl.multiple_of(ids_smem[i, 0, slot] * BLOCK, BLOCK)
            source = rows[pl.ds(start, BLOCK), :]
            block = held(i, pl.ds(pl.multiple_of(slot * BLOCK, BLOCK), BLOCK))
            product = lax.dot_general(
                block, source, (((0,), (0,)), ((), ())), preferred_element_type=jnp.float32
            )
            products.append(jnp.where(slot < live, product, 0.0))
        for u in range(GROUP):
            col = ids_smem[i, 1, first + u]
            owner = col // per_piece
            slot_half = (owner % 2) ^ core
            slot_chip = owner // 2
            start = ((slot_half * chips + slot_chip) * count + i) * piece
            start = pl.multiple_of(start + (col % per_piece) * BLOCK, BLOCK)
            totals[pl.ds(start, BLOCK), :] += products[u]

    each_group(ids_smem, place, chunk, visit)
    size = count * piece
    step = keep.shape[0] // chips
    for side, out in enumerate((keep, send)):
        for q in range(chips):
            here = (side * chips + q) * size
            out[q * step : q * step + size, :] = totals[here : here + size, :].astype(jnp.bfloat16)
            if riders:
                more = step - size
                rider = rider_refs[side][q * more : (q + 1) * more, :]
                out[q * step + size : (q + 1) * step, :] = rider


def pair_kernel(chips, place, keep, taken, *outs):
    rows = outs[0].shape[0]
    for d in range(chips):
        here = pl.ds(pl.multiple_of((place[1] ^ d) * rows, rows), rows)
        total = keep[here, :].astype(jnp.float32) + taken[here, :].astype(jnp.float32)
        outs[d][...] = total.astype(jnp.bfloat16)


def plane_kernel(chips, count, place, *refs):
    parts, outs = refs[:chips], refs[chips:]
    rider = outs[count] if len(outs) > count else None
    rows = outs[0].shape[0] - (rider.shape[0] if rider is not None else 0)

    def total(here):
        value = parts[0][here, :].astype(jnp.float32)
        for part in parts[1:]:
            value += part[here, :].astype(jnp.float32)
        return value.astype(jnp.bfloat16)

    for i in range(count):
        outs[i][:rows, :] = total(slice(i * rows, (i + 1) * rows))
    if rider is not None:
        value = total(slice(count * rows, None))
        rider[...] = value
        for i in range(count):
            outs[i][rows:, :] = value


def join_kernel(teams, place, *refs):
    parts = refs[:teams]
    out, held = refs[teams:]
    width = parts[0].shape[1]
    for d in range(teams):
        held[place[0] ^ d] = parts[d][: held.shape[1], :]
    for d in range(teams):
        out[:, d * width : (d + 1) * width] = held[d]


def call(kernel, name, operands, spaces, out_shapes, scratch, flops, limit, after=()):
    moved = sum(math.prod(x.shape) * x.dtype.itemsize for x in (*operands, *out_shapes))
    specs = [pl.BlockSpec(memory_space=space) for space in spaces]
    specs += [pl.BlockSpec(memory_space=pl.ANY) for _ in after]
    given = len(operands)

    def body(*refs):
        row = lax.axis_index("row")
        place = (lax.axis_index("team"), row // 2, row % 2)
        kernel(place, *refs[:given], *refs[given + len(after) :])

    return pl.pallas_call(
        body,
        name=name,
        in_specs=specs,
        out_specs=[pl.BlockSpec(memory_space=pltpu.VMEM) for _ in out_shapes],
        out_shape=out_shapes,
        scratch_shapes=scratch,
        cost_estimate=pl.CostEstimate(
            flops=flops, bytes_accessed=moved if flops else 0, transcendentals=0
        ),
        compiler_params=pltpu.CompilerParams(vmem_limit_bytes=limit),
    )(*operands, *after)


def gather_lists(mine, teams, gate):
    if teams == 4:
        two = swap(mine, "team", 2)
        one = swap(mine, "team", 1)
        relayed = lax.ppermute(two, "team", [(2, 3), (1, 0)])
        held, _ = lax.optimization_barrier((mine, gate(two, one)))
        middle = lax.ppermute(held, "team", [(1, 2), (2, 1)])
        return [mine, one, two], [middle, relayed]
    early = [mine] + [swap(mine, "team", d) for d in range(1, teams - 1)]
    last = swap(mine, "team", teams - 1)
    return early, [last, last]


def per_device(
    features, weight, table, labels, label_mask, block_vals, block_row, block_col, block_count
):
    slab, width = features.shape
    slots = block_vals.shape[2]
    rows_n = lax.axis_size("row")
    teams = lax.axis_size("team")
    chips = rows_n // 2
    nodes = slab * rows_n
    panel_rows = nodes // teams
    part = width // teams
    share = slab // teams
    piece = panel_rows // rows_n
    team = lax.axis_index("team")
    bf16, f32 = jnp.bfloat16, jnp.float32
    any_space, vmem = pl.ANY, pltpu.VMEM
    padded = lanes(part)
    payload = slots * BLOCK + ID_ROWS

    def shaped(*dims, kind=bf16):
        return jax.ShapeDtypeStruct(dims, kind)

    def id_scratch(count):
        return [
            pltpu.VMEM((count, payload, BLOCK), bf16),
            pltpu.VMEM((count, 8, BLOCK), jnp.int32),
            pltpu.SMEM((count, 8, BLOCK), jnp.int32),
        ]

    list_bytes = payload * BLOCK * 2
    list_flops = 2 * slots * BLOCK * BLOCK * part

    aligned = part % 128 == 0
    prepared = call(
        functools.partial(prepare_kernel, slots),
        "prepare",
        [
            block_vals.reshape(slots * BLOCK, BLOCK),
            block_row.reshape(1, slots),
            block_col.reshape(1, slots),
            block_count,
            *([features] if aligned else []),
        ],
        [pltpu.HBM] * (4 + aligned),
        [shaped(payload, BLOCK)] + [shaped(slab, part)] * aligned,
        [
            pltpu.VMEM((1, slots), jnp.int32),
            pltpu.VMEM((1, slots), jnp.int32),
            pltpu.VMEM((1, 1), jnp.int32),
            pltpu.VMEM((ID_ROWS, BLOCK), f32),
            pltpu.SemaphoreType.DMA((5,)),
        ],
        0,
        60 * MIB,
    )
    mine = prepared[0]
    own = prepared[1] if aligned else lax.dynamic_slice_in_dim(features, team * part, part, 1)
    beside = swap(own, "row", 1)
    near = [own] + [swap(own, "row", 2 * d) for d in range(1, chips)]
    early, late = gather_lists(mine, teams, lambda two, one: one)
    far = [beside] + [swap(value, "row", 1) for value in near[1:]]

    ids = id_scratch(teams - 1)
    begun, late_panel, weight_here, table_here = call(
        functools.partial(early_kernel, chips, teams, slots),
        "early_products",
        [*near, *far, *early, weight, table],
        [any_space] * (2 * chips + teams + 1),
        [
            shaped(slab, part, kind=f32),
            shaped(panel_rows, part),
            shaped(*weight.shape),
            shaped(*table.shape),
        ],
        [
            pltpu.VMEM((nodes, part), bf16),
            *ids,
            pltpu.SemaphoreType.DMA((2 * chips + teams + 1,)),
            pltpu.SemaphoreType.DMA,
        ],
        0,
        (nodes + panel_rows) * padded * 2 + teams * list_bytes + slab * padded * 4 + 4 * MIB,
    )
    ids = id_scratch(1)
    sent = call(
        functools.partial(late_kernel, teams, slots),
        "late_products",
        [*late, begun, late_panel],
        [vmem] * 4,
        [shaped(share, part)] * teams,
        [
            pltpu.VMEM((slab, part), f32),
            *ids,
            pltpu.SemaphoreType.DMA,
        ],
        list_flops,
        (panel_rows + 5 * slab) * padded * 2 + 3 * list_bytes + 3 * MIB,
    )
    aggs = [sent[0]] + [swap(sent[d], "team", d) for d in range(1, teams)]

    output, grad_pre, *backs = call(
        functools.partial(layer_kernel, teams),
        "layer",
        [
            *aggs,
            weight_here,
            table_here,
            labels.reshape(teams, share),
            label_mask.reshape(teams, share),
        ],
        [vmem] * (teams + 2) + [any_space] * 2,
        [shaped(share, width)] * 2 + [shaped(share, part)] * teams,
        [
            pltpu.VMEM((teams, share), jnp.int32),
            pltpu.VMEM((teams, share), jnp.int32),
            pltpu.VMEM((teams, share, part), bf16),
            pltpu.SemaphoreType.DMA((2,)),
        ],
        4 * share * width * width,
        16 * MIB,
    )
    backs = [backs[0]] + [swap(backs[d], "team", d) for d in range(1, teams)]

    half = width // 2
    rider = half // chips * teams
    w_keep, w_send = call(
        functools.partial(weight_kernel, teams, chips),
        "weight_term",
        [*aggs, grad_pre],
        [vmem] * (teams + 1),
        [shaped(chips * rider, part)] * 2,
        [pltpu.VMEM((width, width), bf16)],
        2 * share * width * width,
        12 * MIB,
    )

    def plane_total(pieces):
        return [pieces[0]] + [swap(pieces[d], "row", 2 * d) for d in range(1, chips)]

    chunks = [list(range(teams // 2, teams)), list(range(teams // 2))]
    lists = early + late
    slices = [None] * teams
    held, paired = [], []
    for chunk in chunks:
        count = len(chunk)
        first = chunk is chunks[0]
        rows = chips * count * piece
        moved = rows + first * chips * rider
        given = [lists[d] for d in chunk] + (lists[-1:] if teams - 1 in chunk else [])
        riders = [w_keep, w_send] if first else []
        held.append(
            call(
                functools.partial(
                    backward_kernel, chips, teams, slots, piece, chunk, len(riders)
                ),
                "backward",
                [*given, *backs, *riders],
                [vmem] * (len(given) + teams + len(riders)),
                [shaped(moved, part)] * 2,
                [
                    pltpu.VMEM((slab, part), bf16),
                    pltpu.VMEM((2 * rows, part), f32),
                    *id_scratch(count)[1:],
                    pltpu.SemaphoreType.DMA,
                ],
                count * list_flops,
                rows * padded * 14 + (count + 1) * list_bytes + slab * padded * 4 + 4 * MIB,
                after=[value[0] for value in held],
            )
        )
    mark = [held[1][0]]
    for chunk, (keep, send) in zip(chunks, held):
        moved = keep.shape[0]
        paired.append(
            call(
                functools.partial(pair_kernel, chips),
                "pair_sum",
                [keep, swap(send, "row", 1)],
                [vmem] * 2,
                [shaped(moved // chips, part)] * chips,
                [],
                moved * part,
                moved * padded * 6 + 3 * MIB,
                after=mark,
            )
        )
        mark = paired[0][:1]
    mark = paired[1][:1]
    for chunk, pieces in zip(chunks, paired):
        count = len(chunk)
        first = chunk is chunks[0]
        outs = [shaped(piece + first * rider, part)] * count + [shaped(rider, part)] * first
        sums = call(
            functools.partial(plane_kernel, chips, count),
            "plane_sum",
            plane_total(pieces),
            [vmem] * chips,
            outs,
            [],
            chips * count * piece * part,
            chips * (count * piece + rider) * padded * 4 + 3 * MIB,
            after=mark,
        )
        for d, value in zip(chunk, sums):
            slices[d] = swap(value, "team", d) if d else value
        mark = []
        if first:
            w_plane = sums[count]
    w_parts = [w_plane] + [
        slices[d] if d in chunks[0] else swap(w_plane, "team", d) for d in range(1, teams)
    ]
    (w_total,) = call(
        functools.partial(weight_total_kernel, teams),
        "weight_total",
        w_parts,
        [vmem] * teams,
        [shaped(rider, part)],
        [],
        half * width,
        6 * MIB,
        after=sums[:1],
    )
    w_near = plane_total([w_total] * chips)
    w_far = [swap(value, "row", 1) for value in w_near]
    (grad_weight,) = call(
        functools.partial(whole_kernel, chips, teams, 1.0 / math.sqrt(nodes)),
        "weight_whole",
        [*w_near, *w_far],
        [vmem] * (2 * chips),
        [shaped(width, width, kind=f32)],
        [],
        half * width,
        6 * MIB,
        after=[slices[d] for d in chunks[1][1:]],
    )
    (grad_features,) = call(
        functools.partial(join_kernel, teams),
        "join",
        slices,
        [vmem] * teams,
        [shaped(piece, width)],
        [pltpu.VMEM((teams, piece, part), bf16)],
        piece * width,
        teams * piece * padded * 8 + 3 * MIB,
    )

    return (output, grad_weight, grad_features[None])


def solution(mesh):
    placed = (
        P("row", None),
        P(),
        P(),
        P("row"),
        P("row"),
        P("row", "team", None, None, None),
        P("row", "team", None),
        P("row", "team", None),
        P("row", "team"),
    )
    return jax.shard_map(
        per_device,
        mesh=mesh,
        in_specs=placed,
        out_specs=(P(("row", "team"), None), P(), P("team", "row", None)),
        check_vma=False,
    )
```

```python
import functools
import math

import jax
import jax.numpy as jnp
from jax import lax
from jax.experimental import pallas as pl
from jax.experimental.pallas import tpu as pltpu
from jax.sharding import PartitionSpec as P

BLOCK = 128
GROUP = 4
ID_ROWS = 16
MIB = 1 << 20


def lanes(width):
    return -(-width // 128) * 128


def swap(value, axis, flip):
    size = lax.axis_size(axis)
    return lax.ppermute(value, axis, [(i, i ^ flip) for i in range(size)])


def load_ids(ids_vmem, ids_smem, lists, slots, sem, meanwhile):
    for d in range(lists.shape[0]):
        rows = lists[d, slots * BLOCK :, :].astype(jnp.float32)
        ids_vmem[d] = rows.astype(jnp.int32)[:8]
    copy = pltpu.make_async_copy(ids_vmem, ids_smem, sem)
    copy.start()
    meanwhile()
    copy.wait()


def each_group(ids, place, given, visit):
    for i, d in enumerate(given):
        live = ids[i, 2, 0]

        def step(group, carry, i=i, d=d, live=live):
            visit(i, place[0] ^ d, group * GROUP, live)
            return carry

        lax.fori_loop(0, (live + GROUP - 1) // GROUP, step, 0)


def forward_visit(panels, panel_rows, block_of, ids, totals):
    def visit(i, panel, first, live):
        products = []
        for u in range(GROUP):
            slot = first + u
            start = panel * panel_rows + ids[i, 1, slot] * BLOCK
            source = panels[pl.ds(pl.multiple_of(start, BLOCK), BLOCK), :]
            block = block_of(i, pl.ds(pl.multiple_of(slot * BLOCK, BLOCK), BLOCK))
            product = jnp.dot(block, source, preferred_element_type=jnp.float32)
            products.append(jnp.where(slot < live, product, 0.0))
        for u in range(GROUP):
            start = pl.multiple_of(ids[i, 0, first + u] * BLOCK, BLOCK)
            totals[pl.ds(start, BLOCK), :] += products[u]

    return visit


def prepare_kernel(slots, place, *refs):
    vals, row_ids, col_ids, count = refs[:4]
    rows, cols, lives, tail, sems = refs[-5:]
    mine = refs[4] if len(refs) == 10 else refs[5]
    blocks = slots * BLOCK
    moves = [(row_ids, rows), (col_ids, cols), (count, lives), (vals, mine.at[pl.ds(0, blocks), :])]
    if len(refs) > 10:
        features, near = refs[4], refs[6]
        width = near.shape[1]
        start = pl.multiple_of(place[0] * width, width)
        moves.append((features.at[:, pl.ds(start, width)], near))
    copies = [
        pltpu.make_async_copy(source, target, sems.at[i])
        for i, (source, target) in enumerate(moves)
    ]
    for copy in copies:
        copy.start()
    tail[...] = jnp.zeros_like(tail)
    for copy in copies[:3]:
        copy.wait()
    tail[0:1, 0:slots] = rows[...].astype(jnp.float32)
    tail[1:2, 0:slots] = cols[...].astype(jnp.float32)
    tail[2:3, 0:1] = lives[...].astype(jnp.float32)
    mine[pl.ds(blocks, ID_ROWS), :] = tail[...].astype(jnp.bfloat16)
    for copy in copies[3:]:
        copy.wait()


def early_kernel(chips, teams, slots, place, *refs):
    near = refs[:chips]
    far = refs[chips : 2 * chips]
    early = teams - 1
    given = refs[2 * chips : 2 * chips + early]
    weight, table = refs[2 * chips + early : 2 * chips + early + 2]
    totals, late_panel, *kept = refs[2 * chips + early + 2 : 2 * chips + early + 6]
    panels, lists, ids_vmem, ids_smem, sems, id_sem = refs[2 * chips + early + 6 :]
    slab = near[0].shape[0]
    panel_rows = panels.shape[0] // teams
    team, chip, core = place[0], place[1], place[2]
    copies = []
    for d in range(early):
        copies.append(pltpu.make_async_copy(given[d], lists.at[d], sems.at[d]))
    for d in range(chips):
        for side, source in ((core, near[d]), (1 - core, far[d])):
            start = pl.multiple_of((2 * (chip ^ d) + side) * slab, slab)
            target = panels.at[pl.ds(start, slab), :]
            copies.append(pltpu.make_async_copy(source, target, sems.at[len(copies)]))
    for source, target in zip((weight, table), kept):
        copies.append(pltpu.make_async_copy(source, target, sems.at[len(copies)]))
    for copy in copies:
        copy.start()

    def clear():
        totals[...] = jnp.zeros_like(totals)

    for copy in copies[:early]:
        copy.wait()
    load_ids(ids_vmem, ids_smem, lists, slots, id_sem, clear)
    for copy in copies[early:]:
        copy.wait()
    visit = forward_visit(panels, panel_rows, lambda i, here: lists[i, here, :], ids_smem, totals)
    each_group(ids_smem, place, range(early), visit)
    start = pl.multiple_of((team ^ early) * panel_rows, panel_rows)
    late_panel[...] = panels[pl.ds(start, panel_rows), :]


def pick(place, teams, middle, relayed, here):
    at_end = (place[0] == 0) | (place[0] == teams - 1)
    return jnp.where(at_end, relayed[here, :], middle[here, :])


def late_kernel(teams, slots, place, *refs):
    middle, relayed, begun, panel = refs[:4]
    outs = refs[4 : 4 + teams]
    totals, ids_vmem, ids_smem, id_sem = refs[4 + teams :]
    tail = pick(place, teams, middle, relayed, pl.ds(slots * BLOCK, ID_ROWS))
    ids_vmem[0] = tail.astype(jnp.float32).astype(jnp.int32)[:8]
    copy = pltpu.make_async_copy(ids_vmem, ids_smem, id_sem)
    copy.start()
    totals[...] = begun[...]
    copy.wait()
    late = functools.partial(pick, place, teams, middle, relayed)
    visit = forward_visit(panel, 0, lambda i, here: late(here), ids_smem, totals)
    each_group(ids_smem, place, [teams - 1], visit)
    share = outs[0].shape[0]
    for d in range(teams):
        start = pl.multiple_of((place[0] ^ d) * share, share)
        outs[d][...] = totals[pl.ds(start, share), :].astype(jnp.bfloat16)


def layer_kernel(teams, place, *refs):
    parts = refs[:teams]
    weight, table, *fixed = refs[teams : teams + 4]
    output, grad_pre = refs[teams + 4 : teams + 6]
    backs = refs[teams + 6 : 2 * teams + 6]
    labels, mask, cols, sems = refs[2 * teams + 6 :]
    team = place[0]
    width = parts[0].shape[1]
    copies = [
        pltpu.make_async_copy(source, target, sems.at[i])
        for i, (source, target) in enumerate(zip(fixed, (labels, mask)))
    ]
    for copy in copies:
        copy.start()

    for d in range(teams):
        cols[team ^ d] = parts[d][...]
    agg = jnp.concatenate([cols[t] for t in range(teams)], axis=1)
    preact = jnp.dot(agg, weight[...], preferred_element_type=jnp.float32)
    sigma = 1.0 / (1.0 + jnp.exp(-preact))
    active = preact * sigma
    output[...] = active.astype(jnp.bfloat16)
    classes = table.shape[0]
    for copy in copies:
        copy.wait()
    row_labels = labels[pl.ds(team, 1), :]
    row_mask = mask[pl.ds(team, 1), :].astype(jnp.float32)
    rows = row_labels.shape[1]
    index = lax.broadcasted_iota(jnp.int32, (classes, rows), 0)
    known = jnp.where(index == row_labels, row_mask, 0.0).astype(jnp.bfloat16)
    held = jnp.broadcast_to(row_mask * (1.0 / 8.0), (8, rows)).astype(jnp.bfloat16)
    across = (((0,), (0,)), ((), ()))
    target = lax.dot_general(known, table[...], across, preferred_element_type=jnp.float32)
    ones = jnp.ones((8, table.shape[1]), jnp.bfloat16)
    masked = lax.dot_general(held, ones, across, preferred_element_type=jnp.float32)
    slope = sigma * (1.0 + preact * (1.0 - sigma))
    grad = ((masked * active - target) * slope).astype(jnp.bfloat16)
    grad_pre[...] = grad
    back = lax.dot_general(
        grad, weight[...], (((1,), (1,)), ((), ())), preferred_element_type=jnp.float32
    ).astype(jnp.bfloat16)
    for t in range(teams):
        cols[t] = back[:, t * width : (t + 1) * width]
    for d in range(teams):
        backs[d][...] = cols[team ^ d]


def weight_kernel(teams, chips, place, *refs):
    parts = refs[:teams]
    grad_pre, keep, send, term = refs[teams:]
    width = parts[0].shape[1]
    for d in range(teams):
        start = pl.multiple_of((place[0] ^ d) * width, width)
        term[pl.ds(start, width), :] = lax.dot_general(
            parts[d][...], grad_pre[...], (((0,), (0,)), ((), ())), preferred_element_type=jnp.float32
        ).astype(jnp.bfloat16)
    half = term.shape[0] // 2
    rows = half // chips
    for out, side in ((keep, place[2]), (send, 1 - place[2])):
        for q in range(chips):
            held = pl.ds(pl.multiple_of(side * half + q * rows, rows), rows)
            for t in range(teams):
                start = (q * teams + t) * rows
                out[start : start + rows, :] = term[held, t * width : (t + 1) * width]


def tree(values):
    while len(values) > 1:
        values = [values[i] + values[i + 1] for i in range(0, len(values), 2)]
    return values[0]


def weight_total_kernel(teams, place, *refs):
    out = refs[teams]
    rows = out.shape[0]
    values = [ref[ref.shape[0] - rows :, :].astype(jnp.float32) for ref in refs[:teams]]
    out[...] = tree(values).astype(out.dtype)


def whole_kernel(chips, teams, scale, place, *refs):
    out = refs[2 * chips]
    rows = refs[0].shape[0] // teams
    width = refs[0].shape[1]
    for side, pieces in ((place[2], refs[:chips]), (1 - place[2], refs[chips : 2 * chips])):
        for d in range(chips):
            start = (side * chips + (place[1] ^ d)) * rows
            held = pl.ds(pl.multiple_of(start, rows), rows)
            for t in range(teams):
                value = pieces[d][t * rows : (t + 1) * rows, :].astype(jnp.float32)
                out[held, t * width : (t + 1) * width] = value * scale


def backward_kernel(chips, teams, slots, piece, chunk, riders, place, *refs):
    count = len(chunk)
    last = teams - 1 in chunk
    given = refs[: count + last]
    backs = refs[count + last : count + last + teams]
    refs = refs[count + last + teams :]

    def held(i, here):
        if last and i == count - 1:
            return pick(place, teams, given[i], given[i + 1], here)
        return given[i][here, :]

    rider_refs, refs = refs[:riders], refs[riders:]
    keep, send, rows, totals, ids_vmem, ids_smem, id_sem = refs
    team, core = place[0], place[2]
    share = backs[0].shape[0]
    per_piece = piece // BLOCK
    for i in range(count):
        tail = held(i, pl.ds(slots * BLOCK, ID_ROWS)).astype(jnp.float32)
        ids_vmem[i] = tail.astype(jnp.int32)[:8]
    copy = pltpu.make_async_copy(ids_vmem, ids_smem, id_sem)
    copy.start()
    totals[...] = jnp.zeros_like(totals)
    for d in range(teams):
        start = pl.multiple_of((team ^ d) * share, share)
        rows[pl.ds(start, share), :] = backs[d][...]
    copy.wait()

    def visit(i, panel, first, live):
        products = []
        for u in range(GROUP):
            slot = first + u
            start = pl.multiple_of(ids_smem[i, 0, slot] * BLOCK, BLOCK)
            source = rows[pl.ds(start, BLOCK), :]
            block = held(i, pl.ds(pl.multiple_of(slot * BLOCK, BLOCK), BLOCK))
            product = lax.dot_general(
                block, source, (((0,), (0,)), ((), ())), preferred_element_type=jnp.float32
            )
            products.append(jnp.where(slot < live, product, 0.0))
        for u in range(GROUP):
            col = ids_smem[i, 1, first + u]
            owner = col // per_piece
            slot_half = (owner % 2) ^ core
            slot_chip = owner // 2
            start = ((slot_half * chips + slot_chip) * count + i) * piece
            start = pl.multiple_of(start + (col % per_piece) * BLOCK, BLOCK)
            totals[pl.ds(start, BLOCK), :] += products[u]

    each_group(ids_smem, place, chunk, visit)
    size = count * piece
    step = keep.shape[0] // chips
    for side, out in enumerate((keep, send)):
        for q in range(chips):
            here = (side * chips + q) * size
            out[q * step : q * step + size, :] = totals[here : here + size, :].astype(jnp.bfloat16)
            if riders:
                more = step - size
                rider = rider_refs[side][q * more : (q + 1) * more, :]
                out[q * step + size : (q + 1) * step, :] = rider


def pair_kernel(chips, place, keep, taken, *outs):
    rows = outs[0].shape[0]
    for d in range(chips):
        here = pl.ds(pl.multiple_of((place[1] ^ d) * rows, rows), rows)
        total = keep[here, :].astype(jnp.float32) + taken[here, :].astype(jnp.float32)
        outs[d][...] = total.astype(jnp.bfloat16)


def plane_kernel(chips, count, place, *refs):
    parts, outs = refs[:chips], refs[chips:]
    rider = outs[count] if len(outs) > count else None
    rows = outs[0].shape[0] - (rider.shape[0] if rider is not None else 0)

    def total(here):
        value = parts[0][here, :].astype(jnp.float32)
        for part in parts[1:]:
            value += part[here, :].astype(jnp.float32)
        return value.astype(jnp.bfloat16)

    for i in range(count):
        outs[i][:rows, :] = total(slice(i * rows, (i + 1) * rows))
    if rider is not None:
        value = total(slice(count * rows, None))
        rider[...] = value
        for i in range(count):
            outs[i][rows:, :] = value


def join_kernel(teams, place, *refs):
    parts = refs[:teams]
    out, held = refs[teams:]
    width = parts[0].shape[1]
    for d in range(teams):
        held[place[0] ^ d] = parts[d][: held.shape[1], :]
    for d in range(teams):
        out[:, d * width : (d + 1) * width] = held[d]


def call(kernel, name, operands, spaces, out_shapes, scratch, flops, limit, after=()):
    moved = sum(math.prod(x.shape) * x.dtype.itemsize for x in (*operands, *out_shapes))
    specs = [pl.BlockSpec(memory_space=space) for space in spaces]
    specs += [pl.BlockSpec(memory_space=pl.ANY) for _ in after]
    given = len(operands)

    def body(*refs):
        row = lax.axis_index("row")
        place = (lax.axis_index("team"), row // 2, row % 2)
        kernel(place, *refs[:given], *refs[given + len(after) :])

    return pl.pallas_call(
        body,
        name=name,
        in_specs=specs,
        out_specs=[pl.BlockSpec(memory_space=pltpu.VMEM) for _ in out_shapes],
        out_shape=out_shapes,
        scratch_shapes=scratch,
        cost_estimate=pl.CostEstimate(
            flops=flops, bytes_accessed=moved if flops else 0, transcendentals=0
        ),
        compiler_params=pltpu.CompilerParams(vmem_limit_bytes=limit),
    )(*operands, *after)


def gather_lists(mine, teams, gate):
    if teams == 4:
        two = swap(mine, "team", 2)
        one = swap(mine, "team", 1)
        relayed = lax.ppermute(two, "team", [(2, 3), (1, 0)])
        held, _ = lax.optimization_barrier((mine, gate(two, one)))
        middle = lax.ppermute(held, "team", [(1, 2), (2, 1)])
        return [mine, one, two], [middle, relayed]
    early = [mine] + [swap(mine, "team", d) for d in range(1, teams - 1)]
    last = swap(mine, "team", teams - 1)
    return early, [last, last]


def per_device(
    features, weight, table, labels, label_mask, block_vals, block_row, block_col, block_count
):
    slab, width = features.shape
    slots = block_vals.shape[2]
    rows_n = lax.axis_size("row")
    teams = lax.axis_size("team")
    chips = rows_n // 2
    nodes = slab * rows_n
    panel_rows = nodes // teams
    part = width // teams
    share = slab // teams
    piece = panel_rows // rows_n
    team = lax.axis_index("team")
    bf16, f32 = jnp.bfloat16, jnp.float32
    any_space, vmem = pl.ANY, pltpu.VMEM
    padded = lanes(part)
    payload = slots * BLOCK + ID_ROWS

    def shaped(*dims, kind=bf16):
        return jax.ShapeDtypeStruct(dims, kind)

    def id_scratch(count):
        return [
            pltpu.VMEM((count, payload, BLOCK), bf16),
            pltpu.VMEM((count, 8, BLOCK), jnp.int32),
            pltpu.SMEM((count, 8, BLOCK), jnp.int32),
        ]

    list_bytes = payload * BLOCK * 2
    list_flops = 2 * slots * BLOCK * BLOCK * part

    aligned = part % 128 == 0
    prepared = call(
        functools.partial(prepare_kernel, slots),
        "prepare",
        [
            block_vals.reshape(slots * BLOCK, BLOCK),
            block_row.reshape(1, slots),
            block_col.reshape(1, slots),
            block_count,
            *([features] if aligned else []),
        ],
        [pltpu.HBM] * (4 + aligned),
        [shaped(payload, BLOCK)] + [shaped(slab, part)] * aligned,
        [
            pltpu.VMEM((1, slots), jnp.int32),
            pltpu.VMEM((1, slots), jnp.int32),
            pltpu.VMEM((1, 1), jnp.int32),
            pltpu.VMEM((ID_ROWS, BLOCK), f32),
            pltpu.SemaphoreType.DMA((5,)),
        ],
        0,
        60 * MIB,
    )
    mine = prepared[0]
    own = prepared[1] if aligned else lax.dynamic_slice_in_dim(features, team * part, part, 1)
    beside = swap(own, "row", 1)
    near = [own] + [swap(own, "row", 2 * d) for d in range(1, chips)]
    early, late = gather_lists(mine, teams, lambda two, one: one)
    far = [beside] + [swap(value, "row", 1) for value in near[1:]]

    ids = id_scratch(teams - 1)
    begun, late_panel, weight_here, table_here = call(
        functools.partial(early_kernel, chips, teams, slots),
        "early_products",
        [*near, *far, *early, weight, table],
        [any_space] * (2 * chips + teams + 1),
        [
            shaped(slab, part, kind=f32),
            shaped(panel_rows, part),
            shaped(*weight.shape),
            shaped(*table.shape),
        ],
        [
            pltpu.VMEM((nodes, part), bf16),
            *ids,
            pltpu.SemaphoreType.DMA((2 * chips + teams + 1,)),
            pltpu.SemaphoreType.DMA,
        ],
        0,
        (nodes + panel_rows) * padded * 2 + teams * list_bytes + slab * padded * 4 + 4 * MIB,
    )
    ids = id_scratch(1)
    sent = call(
        functools.partial(late_kernel, teams, slots),
        "late_products",
        [*late, begun, late_panel],
        [vmem] * 4,
        [shaped(share, part)] * teams,
        [
            pltpu.VMEM((slab, part), f32),
            *ids[1:],
            pltpu.SemaphoreType.DMA,
        ],
        list_flops,
        (panel_rows + 5 * slab) * padded * 2 + 3 * list_bytes + 3 * MIB,
    )
    aggs = [sent[0]] + [swap(sent[d], "team", d) for d in range(1, teams)]

    output, grad_pre, *backs = call(
        functools.partial(layer_kernel, teams),
        "layer",
        [
            *aggs,
            weight_here,
            table_here,
            labels.reshape(teams, share),
            label_mask.reshape(teams, share),
        ],
        [vmem] * (teams + 2) + [any_space] * 2,
        [shaped(share, width)] * 2 + [shaped(share, part)] * teams,
        [
            pltpu.VMEM((teams, share), jnp.int32),
            pltpu.VMEM((teams, share), jnp.int32),
            pltpu.VMEM((teams, share, part), bf16),
            pltpu.SemaphoreType.DMA((2,)),
        ],
        4 * share * width * width,
        16 * MIB,
    )
    backs = [backs[0]] + [swap(backs[d], "team", d) for d in range(1, teams)]

    half = width // 2
    rider = half // chips * teams
    w_keep, w_send = call(
        functools.partial(weight_kernel, teams, chips),
        "weight_term",
        [*aggs, grad_pre],
        [vmem] * (teams + 1),
        [shaped(chips * rider, part)] * 2,
        [pltpu.VMEM((width, width), bf16)],
        2 * share * width * width,
        12 * MIB,
    )

    def plane_total(pieces):
        return [pieces[0]] + [swap(pieces[d], "row", 2 * d) for d in range(1, chips)]

    chunks = [list(range(teams // 2, teams)), list(range(teams // 2))]
    lists = early + late
    slices = [None] * teams
    held, paired = [], []
    for chunk in chunks:
        count = len(chunk)
        first = chunk is chunks[0]
        rows = chips * count * piece
        moved = rows + first * chips * rider
        given = [lists[d] for d in chunk] + (lists[-1:] if teams - 1 in chunk else [])
        riders = [w_keep, w_send] if first else []
        held.append(
            call(
                functools.partial(
                    backward_kernel, chips, teams, slots, piece, chunk, len(riders)
                ),
                "backward",
                [*given, *backs, *riders],
                [vmem] * (len(given) + teams + len(riders)),
                [shaped(moved, part)] * 2,
                [
                    pltpu.VMEM((slab, part), bf16),
                    pltpu.VMEM((2 * rows, part), f32),
                    *id_scratch(count)[1:],
                    pltpu.SemaphoreType.DMA,
                ],
                count * list_flops,
                rows * padded * 14 + (count + 1) * list_bytes + slab * padded * 4 + 4 * MIB,
                after=[value[0] for value in held],
            )
        )
    mark = [held[1][0]]
    for chunk, (keep, send) in zip(chunks, held):
        moved = keep.shape[0]
        paired.append(
            call(
                functools.partial(pair_kernel, chips),
                "pair_sum",
                [keep, swap(send, "row", 1)],
                [vmem] * 2,
                [shaped(moved // chips, part)] * chips,
                [],
                moved * part,
                moved * padded * 6 + 3 * MIB,
                after=mark,
            )
        )
        mark = paired[0][:1]
    mark = paired[1][:1]
    for chunk, pieces in zip(chunks, paired):
        count = len(chunk)
        first = chunk is chunks[0]
        outs = [shaped(piece + first * rider, part)] * count + [shaped(rider, part)] * first
        sums = call(
            functools.partial(plane_kernel, chips, count),
            "plane_sum",
            plane_total(pieces),
            [vmem] * chips,
            outs,
            [],
            chips * count * piece * part,
            chips * (count * piece + rider) * padded * 4 + 3 * MIB,
            after=mark,
        )
        for d, value in zip(chunk, sums):
            slices[d] = swap(value, "team", d) if d else value
        mark = []
        if first:
            w_plane = sums[count]
    w_parts = [w_plane] + [
        slices[d] if d in chunks[0] else swap(w_plane, "team", d) for d in range(1, teams)
    ]
    (w_total,) = call(
        functools.partial(weight_total_kernel, teams),
        "weight_total",
        w_parts,
        [vmem] * teams,
        [shaped(rider, part)],
        [],
        half * width,
        6 * MIB,
        after=sums[:1],
    )
    w_near = plane_total([w_total] * chips)
    w_far = [swap(value, "row", 1) for value in w_near]
    (grad_weight,) = call(
        functools.partial(whole_kernel, chips, teams, 1.0 / math.sqrt(nodes)),
        "weight_whole",
        [*w_near, *w_far],
        [vmem] * (2 * chips),
        [shaped(width, width, kind=f32)],
        [],
        half * width,
        6 * MIB,
        after=[slices[d] for d in chunks[1][1:]],
    )
    (grad_features,) = call(
        functools.partial(join_kernel, teams),
        "join",
        slices,
        [vmem] * teams,
        [shaped(piece, width)],
        [pltpu.VMEM((teams, piece, part), bf16)],
        piece * width,
        teams * piece * padded * 8 + 3 * MIB,
    )

    return (output, grad_weight, grad_features[None])


def solution(mesh):
    placed = (
        P("row", None),
        P(),
        P(),
        P("row"),
        P("row"),
        P("row", "team", None, None, None),
        P("row", "team", None),
        P("row", "team", None),
        P("row", "team"),
    )
    return jax.shard_map(
        per_device,
        mesh=mesh,
        in_specs=placed,
        out_specs=(P(("row", "team"), None), P(), P("team", "row", None)),
        check_vma=False,
    )
```
